32 devices in a mesh: space: 16 (over z, y, x), load: 2 (over core).
Axes of the slice: x: 2, y: 2, z: 4, core: 2. Of those that a mesh axis runs over, the one named last changes fastest.
Arguments:
- forward_disp: float32 [2, 3, 32, 128, 128], P('load', None, 'space'), may hold values from -6 to 6
- adjoint_rhs: float32 [2, 3, 32, 128, 128], P('load', None, 'space'), may hold values from -72 to 72
- modulus_factor: float32 [32, 128, 128], P('space'), may hold values from 0.5 to 2
- zone_base: float32 [8], replicated, may hold values from 0.3 to 3
- zone_ids: int32 [32, 128, 128], P('space'), may hold values from 0 to 7
- fixed_mask: int32 [32, 128, 128], P('space'), may hold values 0 or 1
Outputs:
- adjoint_disp: float32 [2, 3, 32, 128, 128], P('load', None, 'space')
- modulus_grad: float32 [32, 128, 128], P('space', 'load')
The draws below stay inside these ranges and needn't reach their ends.
All inputs are finite; a program needn't handle non-finite values. No bound on the sum of `fixed_mask` on one device may be relied on, other than what follows from the above.
Results may differ from the reference program's by a relative error of at most 0.00016.
Values sent between devices are 32-bit elements; how exact they have to be, the bound alone decides.
No kernel may reach another device: no remote copies, remote signals or barrier semaphores. Data moves between devices by JAX's collectives and lax.ppermute only.
A program may use at most 64 MiB of HBM per device.

```python
import math
import jax
import jax.numpy as jnp
import numpy as np
from jax import lax

NX = 128
NY = 128
ZONES = 8
ITERS = 2
NZ = 32
LOADS = 2


def draw_adjoint_rhs(key, part):
    keys = jax.random.split(jax.random.fold_in(key, 17), 3)
    shape = (LOADS, 3, NZ, NY, NX)
    depth = (jnp.arange(NZ, dtype=jnp.float32) + 0.5) / NZ - 0.5
    spread = math.log(10.0) / 2.0
    rows = jnp.exp(jax.random.uniform(keys[1], (NY,), jnp.float32, -spread, spread))
    columns = jnp.exp(jax.random.uniform(keys[2], (NX,), jnp.float32, -spread, spread))
    base = jnp.clip(jax.random.normal(keys[0], shape, jnp.float32), -4.0, 4.0)
    rising = jnp.exp(math.log(3.0) * depth)
    values = base * rising[:, None, None] * rows[:, None] * columns[None, :]
    return values


def set_ends(array, key, least, largest):
    shape = array.shape
    index_at = [jax.random.randint(jax.random.fold_in(key, axis), (), 0, shape[axis]) for axis in range(len(shape))]
    array = array.at[tuple(index_at)].set(least)
    longest = shape.index(max(shape))
    index_at[longest] = (index_at[longest] + 1) % shape[longest]
    return array.at[tuple(index_at)].set(largest)


def block_levels(own_key, dims, cuts, low, largest):
    loudness, own = 1.0, jax.random.fold_in(own_key, 6)
    for dim, blocks in cuts:
        steps = jnp.exp(jax.random.uniform(jax.random.fold_in(own, dim), (blocks,), jnp.float32, low / len(cuts), largest / len(cuts)))
        loudness = loudness * jnp.repeat(steps, dims[dim] // blocks).reshape([-1 if axis == dim else 1 for axis in range(len(dims))])
    return loudness


def bell_draw(key, extent, scale, limit, cuts=(), held_as=jnp.bfloat16):
    factor_of = block_levels(key, extent, cuts, -0.22, 0.18) if cuts else 1.0
    result = jax.random.normal(key, extent, jnp.float32) * scale * factor_of
    return jnp.minimum(jnp.maximum(result, -limit), limit).astype(held_as)


def setup_inputs(seed: int = 0) -> dict:
    splits = jax.random.split(jax.random.key(seed), 7)
    forward_disp = bell_draw(splits[0], (LOADS, 3, NZ, NY, NX), 1.0, 6.0, ((0, 2), (2, 16)), jnp.float32)
    adjoint_rhs = draw_adjoint_rhs(jax.random.fold_in(splits[6], 71), 0)
    modulus_factor = jnp.clip(jnp.exp(math.log(2.0) - 1.3862944 * jax.random.uniform(splits[2], (NZ, NY, NX), jnp.float32) ** block_levels(splits[2], (NZ, NY, NX), ((0, 16),), -0.2, 0.2)), 0.5, 2.0)
    zone_base = jnp.clip(jnp.exp(jax.random.uniform(splits[3], (ZONES,), jnp.float32, math.log(0.3), math.log(3.0))), 0.3, 3.0)
    zone_ids = set_ends(jax.random.randint(splits[4], (NZ, NY, NX), 0, ZONES), jax.random.fold_in(splits[4], 1), 0, ZONES - 1).astype(jnp.int32)
    fixed_mask = set_ends((jax.random.randint(splits[5], (NZ, NY, NX), 0, 8) < 1).astype(jnp.int32), jax.random.fold_in(splits[5], 1), 0, 1)
    return {"forward_disp": forward_disp, "adjoint_rhs": adjoint_rhs, "modulus_factor": modulus_factor, "zone_base": zone_base, "zone_ids": zone_ids, "fixed_mask": fixed_mask}


def unit_stiffness():
    poisson = 0.3
    lame_first = poisson / ((1.0 + poisson) * (1.0 - 2.0 * poisson))
    shear_mod = 0.5 / (1.0 + poisson)
    elastic = np.zeros((6, 6))
    elastic[:3, :3] = lame_first
    for index in range(3):
        elastic[index, index] += 2.0 * shear_mod
        elastic[index + 3, index + 3] = shear_mod
    points = [0.5 - 0.5 / np.sqrt(3.0), 0.5 + 0.5 / np.sqrt(3.0)]
    stiffness = np.zeros((24, 24))
    for point_z in points:
        for point_y in points:
            for point_x in points:
                gradient = np.zeros((3, 8))
                for corner in range(8):
                    off_z, off_y, off_x = (corner // 4, corner // 2 % 2, corner % 2)
                    shape_x = point_x if off_x else 1.0 - point_x
                    shape_y = point_y if off_y else 1.0 - point_y
                    shape_z = point_z if off_z else 1.0 - point_z
                    sign_x = 1.0 if off_x else -1.0
                    sign_y = 1.0 if off_y else -1.0
                    sign_z = 1.0 if off_z else -1.0
                    gradient[0, corner] = sign_x * shape_y * shape_z
                    gradient[1, corner] = shape_x * sign_y * shape_z
                    gradient[2, corner] = shape_x * shape_y * sign_z
                strain_map = np.zeros((6, 24))
                for corner in range(8):
                    strain_map[0, corner] = gradient[0, corner]
                    strain_map[1, 8 + corner] = gradient[1, corner]
                    strain_map[2, 16 + corner] = gradient[2, corner]
                    strain_map[3, corner] = gradient[1, corner]
                    strain_map[3, 8 + corner] = gradient[0, corner]
                    strain_map[4, 8 + corner] = gradient[2, corner]
                    strain_map[4, 16 + corner] = gradient[1, corner]
                    strain_map[5, 16 + corner] = gradient[0, corner]
                    strain_map[5, corner] = gradient[2, corner]
                stiffness += strain_map.T @ elastic @ strain_map / 8.0
    return stiffness

def corner_offsets(corner):
    return (corner // 4, corner // 2 % 2, corner % 2)

def element_vectors(extended):
    lead = extended.ndim - 4
    padded = jnp.pad(extended, [(0, 0)] * (lead + 2) + [(0, 1), (0, 1)])
    layers = extended.shape[-3] - 1
    height = extended.shape[-2]
    width = extended.shape[-1]
    pieces = []
    for corner in range(8):
        off_z, off_y, off_x = corner_offsets(corner)
        pieces.append(padded[..., off_z:off_z + layers, off_y:off_y + height, off_x:off_x + width])
    stacked = jnp.stack(pieces, axis=-4)
    return stacked.reshape(stacked.shape[:lead] + (24, layers, height, width))

def stiff_product(vectors, stiffness):
    return jnp.einsum('ab,...bzyx->...azyx', stiffness, vectors, precision=lax.Precision.HIGHEST)

def assemble(forces):
    lead = forces.ndim - 4
    layers, height, width = forces.shape[-3:]
    split = forces.reshape(forces.shape[:lead] + (3, 8, layers, height, width))
    total = None
    for corner in range(8):
        off_z, off_y, off_x = corner_offsets(corner)
        placed = jnp.pad(split[..., corner, :, :, :], [(0, 0)] * (lead + 1) + [(off_z, 1 - off_z), (off_y, 1 - off_y), (off_x, 1 - off_x)])
        total = placed if total is None else total + placed
    return total[..., :height, :width]

def node_diagonal(padded, layers, height, width):
    total = None
    for corner in range(8):
        off_z, off_y, off_x = corner_offsets(corner)
        piece = padded[1 - off_z:1 - off_z + layers, 1 - off_y:1 - off_y + height, 1 - off_x:1 - off_x + width]
        total = piece if total is None else total + piece
    return total

def reference(forward_disp, adjoint_rhs, modulus_factor, zone_base, zone_ids, fixed_mask):
    stiffness = jnp.asarray(unit_stiffness(), jnp.float32)
    zone_scale = zone_base[zone_ids]
    modulus = modulus_factor * zone_scale
    free = (1 - fixed_mask).astype(jnp.float32)
    padded = jnp.pad(modulus, ((1, 0), (1, 0), (1, 0)))
    diagonal = node_diagonal(padded, NZ, NY, NX) * stiffness[0, 0]
    inverse = free / diagonal

    def extend(field):
        return jnp.pad(field, ((0, 0), (0, 1), (0, 0), (0, 0)))

    def operate(field):
        forces = stiff_product(element_vectors(extend(field)), stiffness) * modulus
        return free * assemble(forces)[:, :NZ]

    def solve_case(total, pair):
        rhs, forward = pair
        residual = free * rhs
        precond = inverse * residual
        direction = precond
        norm_now = jnp.sum(residual * precond)
        solution = jnp.zeros_like(residual)
        for iteration in range(ITERS):
            image = operate(direction)
            step_size = norm_now / jnp.sum(direction * image)
            solution = solution + step_size * direction
            residual = residual - step_size * image
            precond = inverse * residual
            norm_next = jnp.sum(residual * precond)
            direction = precond + norm_next / norm_now * direction
            norm_now = norm_next
        forward_vec = element_vectors(extend(forward))
        solution_vec = element_vectors(extend(solution))
        term = lax.optimization_barrier(jnp.sum(solution_vec * stiff_product(forward_vec, stiffness), axis=0))
        return (total + term, solution)
    grad_sum, adjoint = lax.scan(solve_case, jnp.zeros((NZ, NY, NX), jnp.float32), (adjoint_rhs, forward_disp))
    return (adjoint, zone_scale * grad_sum)
```

```python
import functools

import jax
import jax.numpy as jnp
from jax import lax
from jax.experimental import pallas as pl
from jax.experimental.pallas import tpu as pltpu
from jax.sharding import PartitionSpec as P

POISSON = 0.3
SHEAR = 0.5 / (1.0 + POISSON)
RATIO = 2.0 * POISSON / (1.0 - 2.0 * POISSON)
CLASS = [0.0] + [12.0 * SHEAR / 64.0 / 3.0**order for order in (1, 2, 3)]
CORNER = CLASS[1] * (RATIO + 4.0) + CLASS[2] * (2.0 * (RATIO + 3.0) + 2.0) + CLASS[3] * (RATIO + 4.0)
ROWS = 8


def permute(shard, axis, by, wrap=False):
    devices = lax.axis_size(axis)
    if wrap:
        pairs = [(i, (i + by) % devices) for i in range(devices)]
    else:
        pairs = [(i, i + by) for i in range(devices) if 0 <= i + by < devices]
    return lax.ppermute(shard, axis, pairs)


def next_lane(value):
    width = value.shape[-1]
    lane = lax.broadcasted_iota(jnp.int32, value.shape, value.ndim - 1)
    return jnp.where(lane == width - 1, 0.0, pltpu.roll(value, width - 1, value.ndim - 1))


def last_lane(value):
    lane = lax.broadcasted_iota(jnp.int32, value.shape, value.ndim - 1)
    return jnp.where(lane == 0, 0.0, pltpu.roll(value, 1, value.ndim - 1))


def store_pair(ref, at, rows, value):
    after = next_lane(value)
    ref[at + (0, rows)] = value + after
    ref[at + (1, rows)] = after - value


def plane_modes(ref, plane, start):
    out = []
    for comp in range(3):
        per = []
        for along in range(2):
            here = ref[plane, comp, along, pl.ds(start, ROWS), :]
            below = ref[plane, comp, along, pl.ds(start + 1, ROWS), :]
            per.append((here + below, below - here))
        out.append(per)
    return out


def layer_modes(low, high):
    out = []
    for comp in range(3):
        modes = {}
        for a in range(2):
            for b in range(2):
                if a or b:
                    modes[a, b, 0] = low[comp][a][b] + high[comp][a][b]
                modes[a, b, 1] = high[comp][a][b] - low[comp][a][b]
        out.append(modes)
    return out


PAIRS = (((0, (1, 1, 0)), (2, (0, 1, 1))), ((1, (1, 1, 0)), (2, (1, 0, 1))), ((0, (1, 0, 1)), (1, (0, 1, 1))))


def stiff(modes):
    u, v, w = modes
    out = [{}, {}, {}]
    trace = RATIO * (u[1, 0, 0] + v[0, 1, 0] + w[0, 0, 1])
    out[0][1, 0, 0] = trace + 2.0 * u[1, 0, 0]
    out[1][0, 1, 0] = trace + 2.0 * v[0, 1, 0]
    out[2][0, 0, 1] = trace + 2.0 * w[0, 0, 1]
    for (one, at), (two, by) in PAIRS:
        both = RATIO * (modes[one][at] + modes[two][by])
        out[one][at] = both + 3.0 * modes[one][at]
        out[two][by] = both + 3.0 * modes[two][by]
    out[0][0, 1, 0] = out[1][1, 0, 0] = u[0, 1, 0] + v[1, 0, 0]
    out[1][0, 0, 1] = out[2][0, 1, 0] = v[0, 0, 1] + w[0, 1, 0]
    out[2][1, 0, 0] = out[0][0, 0, 1] = w[1, 0, 0] + u[0, 0, 1]
    first = u[0, 1, 1] + v[1, 0, 1]
    second = v[1, 0, 1] + w[1, 1, 0]
    third = w[1, 1, 0] + u[0, 1, 1]
    out[0][0, 1, 1] = first + third
    out[1][1, 0, 1] = first + second
    out[2][1, 1, 0] = second + third
    for comp in range(3):
        out[comp][1, 1, 1] = (RATIO + 4.0) * modes[comp][1, 1, 1]
    return out


def paired(modes, forces):
    total = None
    for order in (1, 2, 3):
        part = None
        for comp in range(3):
            for key, force in forces[comp].items():
                if sum(key) == order:
                    term = modes[comp][key] * force
                    part = term if part is None else part + term
        part = CLASS[order] * part
        total = part if total is None else total + part
    return total


def pack_kernel(base_ref, rhs_ref, factor_ref, ids_ref, mask_ref, up_ref, down_ref, res_ref, mod_ref, scale_ref):
    layers, height, width = factor_ref.shape
    ids = ids_ref[...]
    scale = jnp.zeros(ids.shape, jnp.float32)
    for zone in range(base_ref.shape[0]):
        scale = jnp.where(ids == zone, base_ref[zone], scale)
    modulus = factor_ref[...] * scale
    scale_ref[...] = scale
    mod_ref[...] = modulus
    free = 1.0 - mask_ref[...].astype(jnp.float32)
    res = free[None] * rhs_ref[0]
    res_ref[...] = res
    row = lax.broadcasted_iota(jnp.int32, (height, width), 0)

    def inverse(lower, upper, free):
        total = lower + upper
        total = total + last_lane(total)
        total = total + jnp.where(row == 0, 0.0, pltpu.roll(total, 1, 0))
        return free / (CORNER * total)

    high = res[:, layers - 1] * inverse(modulus[layers - 2], modulus[layers - 1], free[layers - 1])
    up_ref[0:3] = high
    up_ref[3] = modulus[layers - 1]
    second = high if layers == 2 else res[:, 1] * inverse(modulus[0], modulus[1], free[1])
    down_ref[0:3] = res[:, 0]
    down_ref[3:6] = second
    down_ref[6] = modulus[0]
    down_ref[7] = free[0]


def image_kernel(
    mask_ref, up_ref, down_ref, res_ref, mod_ref, z_ref, v_ref, sums_ref, z_pair, v_pair, carry, edge, inv
):
    layers, height, width = mod_ref.shape
    blocks = height // ROWS

    def modulus(layer, rows):
        if layer < 0:
            return up_ref[3, rows, :]
        return mod_ref[layer, rows, :] if layer < layers else down_ref[6, rows, :]

    edge[:, 0:ROWS, :] = jnp.zeros((layers + 1, ROWS, width), jnp.float32)
    z_pair[:, :, :, height : height + ROWS, :] = jnp.zeros((layers + 3, 3, 2, ROWS, width), jnp.float32)
    v_pair[:, :, :, height : height + ROWS, :] = jnp.zeros((layers + 1, 3, 2, ROWS, width), jnp.float32)
    carry[:, :, :, 0:ROWS, :] = jnp.zeros((layers + 1, 3, 2, ROWS, width), jnp.float32)

    def start_block(block, norm):
        start = pl.multiple_of(block * ROWS, ROWS)
        rows = pl.ds(start, ROWS)
        for plane in range(layers + 1):
            total = modulus(plane - 1, rows) + modulus(plane, rows)
            total = total + last_lane(total)
            edge[plane, pl.ds(start + ROWS, ROWS), :] = total
            total = total + edge[plane, pl.ds(start + ROWS - 1, ROWS), :]
            free = down_ref[7, rows, :] if plane == layers else 1.0 - mask_ref[plane, rows, :].astype(jnp.float32)
            inverse = free / (CORNER * total)
            inv[plane, rows, :] = inverse
            for comp in range(3):
                res = res_ref[comp, plane, rows, :] if plane < layers else down_ref[comp, rows, :]
                z = inverse * res
                z_ref[comp, plane, rows, :] = z
                store_pair(z_pair, (plane + 1, comp), rows, z)
                if plane < layers:
                    norm = norm + res * z
        for comp in range(3):
            store_pair(z_pair, (0, comp), rows, up_ref[comp, rows, :])
            store_pair(z_pair, (layers + 2, comp), rows, down_ref[3 + comp, rows, :])
        return norm

    zero = jnp.zeros((ROWS, width), jnp.float32)
    norm = lax.fori_loop(0, blocks, start_block, zero)

    def image_block(block, sums):
        along, across = sums
        start = pl.multiple_of(block * ROWS, ROWS)
        rows = pl.ds(start, ROWS)
        low = plane_modes(z_pair, 0, start)
        held = None
        for layer in range(layers + 2):
            high = plane_modes(z_pair, layer + 1, start)
            forces = stiff(layer_modes(low, high))
            stiffness = modulus(layer - 1, rows)
            weight = [None] + [CLASS[order] * stiffness for order in (1, 2, 3)]
            lower, upper = {}, {}
            for comp in range(3):
                for a in range(2):
                    for b in range(2):
                        change = weight[a + b + 1] * forces[comp][a, b, 1]
                        if a or b:
                            level = weight[a + b] * forces[comp][a, b, 0]
                            lower[comp, a, b] = level - change
                            upper[comp, a, b] = level + change
                        else:
                            lower[comp, a, b] = -change
                            upper[comp, a, b] = change
            if layer > 0:
                plane = layer - 1
                inverse = inv[plane, rows, :]
                for comp in range(3):
                    sides = []
                    for a in range(2):
                        level = held[comp, a, 0] + lower[comp, a, 0]
                        change = held[comp, a, 1] + lower[comp, a, 1]
                        carry[plane, comp, a, pl.ds(start + 1, ROWS), :] = level + change
                        sides.append(level - change + carry[plane, comp, a, rows, :])
                    image = sides[0] - sides[1] + last_lane(sides[0] + sides[1])
                    v = inverse * image
                    v_ref[comp, plane, rows, :] = v
                    store_pair(v_pair, (plane, comp), rows, v)
                    if plane < layers:
                        along = along + image * z_ref[comp, plane, rows, :]
                        across = across + image * v
            held = upper
            low = high
        return along, across

    along, across = lax.fori_loop(0, blocks, image_block, (zero, zero))

    def energy_block(block, energy):
        start = pl.multiple_of(block * ROWS, ROWS)
        low = plane_modes(v_pair, 0, start)
        for layer in range(layers):
            high = plane_modes(v_pair, layer + 1, start)
            modes = layer_modes(low, high)
            energy = energy + mod_ref[layer, pl.ds(start, ROWS), :] * paired(modes, stiff(modes))
            low = high
        return energy

    energy = lax.fori_loop(0, blocks, energy_block, zero)
    lane = lax.broadcasted_iota(jnp.int32, sums_ref.shape, 1)
    out = jnp.zeros(sums_ref.shape, jnp.float32)
    for place, part in enumerate((norm, along, across, energy)):
        out = jnp.where(lane == place, jnp.sum(part), out)
    sums_ref[...] = out


def finish_kernel(load_ref, sums_ref, z_ref, v_ref, disp_ref, above_ref, scale_ref, x_ref, grad_ref, x_pair, u_pair):
    layers, height, width = scale_ref.shape
    blocks = height // ROWS
    loads = load_ref[1]
    device = lax.broadcasted_iota(jnp.int32, sums_ref.shape, 0)
    lane = lax.broadcasted_iota(jnp.int32, sums_ref.shape, 1)
    mine = jnp.where(lax.rem(device, loads) == load_ref[0], sums_ref[...], 0.0)
    norm, along, across, energy = [jnp.sum(jnp.where(lane == place, mine, 0.0)) for place in range(4)]
    tail = (ROWS, width)
    norm, along, across, energy = [jnp.full(tail, part) for part in (norm, along, across, energy)]
    first = norm / along
    later = first * first * across - norm
    second = later / (first * first * (energy - across * across / along))
    from_z = first + second * (first * across / along)
    from_v = second * first
    x_pair[:, :, :, height : height + ROWS, :] = jnp.zeros((layers + 1, 3, 2, ROWS, width), jnp.float32)
    u_pair[:, :, :, height : height + ROWS, :] = jnp.zeros((layers + 1, 3, 2, ROWS, width), jnp.float32)

    def combine_block(block, _):
        rows = pl.ds(pl.multiple_of(block * ROWS, ROWS), ROWS)
        for comp in range(3):
            for plane in range(layers + 1):
                x = from_z * z_ref[comp, plane, rows, :] - from_v * v_ref[comp, plane, rows, :]
                if plane < layers:
                    x_ref[0, comp, plane, rows, :] = x
                store_pair(x_pair, (plane, comp), rows, x)
                u = disp_ref[0, comp, plane, rows, :] if plane < layers else above_ref[comp, rows, :]
                store_pair(u_pair, (plane, comp), rows, u)
        return 0

    lax.fori_loop(0, blocks, combine_block, 0)

    def grad_block(block, _):
        start = pl.multiple_of(block * ROWS, ROWS)
        rows = pl.ds(start, ROWS)
        x_low = plane_modes(x_pair, 0, start)
        u_low = plane_modes(u_pair, 0, start)
        for layer in range(layers):
            x_high = plane_modes(x_pair, layer + 1, start)
            u_high = plane_modes(u_pair, layer + 1, start)
            term = paired(layer_modes(x_low, x_high), stiff(layer_modes(u_low, u_high)))
            grad_ref[layer, rows, :] = term * scale_ref[layer, rows, :]
            x_low, u_low = x_high, u_high
        return 0

    lax.fori_loop(0, blocks, grad_block, 0)


def f32(*shape):
    return jax.ShapeDtypeStruct(shape, jnp.float32)


def shards(forward_disp, adjoint_rhs, modulus_factor, zone_base, zone_ids, fixed_mask):
    layers, height, width = modulus_factor.shape
    loads = lax.axis_size("load")
    devices = lax.axis_size("space") * loads
    load = lax.axis_index("load")
    whole = pl.BlockSpec(memory_space=pltpu.VMEM)
    scalar = pl.BlockSpec(memory_space=pltpu.SMEM)
    params = pltpu.CompilerParams(vmem_limit_bytes=32 * 2**20)
    pad = height + ROWS

    up, down, res, modulus, scale = pl.pallas_call(
        pack_kernel,
        out_shape=(
            f32(4, height, width),
            f32(8, height, width),
            f32(3, layers, height, width),
            f32(layers, height, width),
            f32(layers, height, width),
        ),
        in_specs=[scalar] + [whole] * 4,
        out_specs=[whole] * 5,
        compiler_params=params,
        name="pack",
    )(zone_base, adjoint_rhs, modulus_factor, zone_ids, fixed_mask)
    from_below = permute(up, "space", 1)
    from_above = permute(down, "space", -1)
    above_disp = permute(forward_disp[0, :, 0], "space", -1)

    z, v, sums = pl.pallas_call(
        image_kernel,
        out_shape=(
            f32(3, layers + 1, height, width),
            f32(3, layers + 1, height, width),
            f32(devices, 128),
        ),
        in_specs=[whole] * 5,
        out_specs=[whole] * 3,
        scratch_shapes=[
            pltpu.VMEM((layers + 3, 3, 2, pad, width), jnp.float32),
            pltpu.VMEM((layers + 1, 3, 2, pad, width), jnp.float32),
            pltpu.VMEM((layers + 1, 3, 2, pad, width), jnp.float32),
            pltpu.VMEM((layers + 1, pad, width), jnp.float32),
            pltpu.VMEM((layers + 1, height, width), jnp.float32),
        ],
        compiler_params=params,
        name="image",
    )(fixed_mask, from_below, from_above, res, modulus)
    sums = lax.all_to_all(sums, ("space", "load"), 0, 0, tiled=True)

    solution, grad = pl.pallas_call(
        finish_kernel,
        out_shape=(f32(1, 3, layers, height, width), f32(layers, height, width)),
        in_specs=[scalar] + [whole] * 6,
        out_specs=[whole] * 2,
        scratch_shapes=[
            pltpu.VMEM((layers + 1, 3, 2, pad, width), jnp.float32),
            pltpu.VMEM((layers + 1, 3, 2, pad, width), jnp.float32),
        ],
        compiler_params=params,
        name="finish",
    )(jnp.stack([load, loads]).astype(jnp.int32), sums, z, v, forward_disp, above_disp, scale)
    share = height // loads
    total = lax.dynamic_slice_in_dim(grad, load * share, share, 1)
    for by in range(1, loads):
        other = lax.dynamic_slice_in_dim(grad, (load + by) % loads * share, share, 1)
        total = total + permute(other, "load", by, wrap=True)
    return (solution, total)


def solution(mesh):
    placed = (
        P("load", None, "space", None, None),
        P("load", None, "space", None, None),
        P("space", None, None),
        P(),
        P("space", None, None),
        P("space", None, None),
    )
    return jax.shard_map(
        shards,
        mesh=mesh,
        in_specs=placed,
        out_specs=(P("load", None, "space", None, None), P("space", "load", None)),
        check_vma=False,
    )
```

```python
import functools

import jax
import jax.numpy as jnp
from jax import lax
from jax.experimental import pallas as pl
from jax.experimental.pallas import tpu as pltpu
from jax.sharding import PartitionSpec as P

POISSON = 0.3
SHEAR = 0.5 / (1.0 + POISSON)
RATIO = 2.0 * POISSON / (1.0 - 2.0 * POISSON)
CLASS = [0.0] + [12.0 * SHEAR / 64.0 / 3.0**order for order in (1, 2, 3)]
CORNER = CLASS[1] * (RATIO + 4.0) + CLASS[2] * (2.0 * (RATIO + 3.0) + 2.0) + CLASS[3] * (RATIO + 4.0)
ROWS = 64


def permute(shard, axis, by, wrap=False):
    devices = lax.axis_size(axis)
    if wrap:
        pairs = [(i, (i + by) % devices) for i in range(devices)]
    else:
        pairs = [(i, i + by) for i in range(devices) if 0 <= i + by < devices]
    return lax.ppermute(shard, axis, pairs)


def next_lane(value):
    width = value.shape[-1]
    lane = lax.broadcasted_iota(jnp.int32, value.shape, value.ndim - 1)
    return jnp.where(lane == width - 1, 0.0, pltpu.roll(value, width - 1, value.ndim - 1))


def last_lane(value):
    lane = lax.broadcasted_iota(jnp.int32, value.shape, value.ndim - 1)
    return jnp.where(lane == 0, 0.0, pltpu.roll(value, 1, value.ndim - 1))


def plane_modes(ref, plane, start):
    out = []
    for comp in range(3):
        here = ref[plane, comp, pl.ds(start, ROWS), :]
        below = ref[plane, comp, pl.ds(start + 1, ROWS), :]
        level, change = here + below, below - here
        level_next, change_next = next_lane(level), next_lane(change)
        out.append(((level + level_next, change + change_next), (level_next - level, change_next - change)))
    return out


def layer_modes(low, high):
    out = []
    for comp in range(3):
        modes = {}
        for a in range(2):
            for b in range(2):
                if a or b:
                    modes[a, b, 0] = low[comp][a][b] + high[comp][a][b]
                modes[a, b, 1] = high[comp][a][b] - low[comp][a][b]
        out.append(modes)
    return out


PAIRS = (((0, (1, 1, 0)), (2, (0, 1, 1))), ((1, (1, 1, 0)), (2, (1, 0, 1))), ((0, (1, 0, 1)), (1, (0, 1, 1))))


def stiff(modes):
    u, v, w = modes
    out = [{}, {}, {}]
    trace = RATIO * (u[1, 0, 0] + v[0, 1, 0] + w[0, 0, 1])
    out[0][1, 0, 0] = trace + 2.0 * u[1, 0, 0]
    out[1][0, 1, 0] = trace + 2.0 * v[0, 1, 0]
    out[2][0, 0, 1] = trace + 2.0 * w[0, 0, 1]
    for (one, at), (two, by) in PAIRS:
        both = RATIO * (modes[one][at] + modes[two][by])
        out[one][at] = both + 3.0 * modes[one][at]
        out[two][by] = both + 3.0 * modes[two][by]
    out[0][0, 1, 0] = out[1][1, 0, 0] = u[0, 1, 0] + v[1, 0, 0]
    out[1][0, 0, 1] = out[2][0, 1, 0] = v[0, 0, 1] + w[0, 1, 0]
    out[2][1, 0, 0] = out[0][0, 0, 1] = w[1, 0, 0] + u[0, 0, 1]
    first = u[0, 1, 1] + v[1, 0, 1]
    second = v[1, 0, 1] + w[1, 1, 0]
    third = w[1, 1, 0] + u[0, 1, 1]
    out[0][0, 1, 1] = first + third
    out[1][1, 0, 1] = first + second
    out[2][1, 1, 0] = second + third
    for comp in range(3):
        out[comp][1, 1, 1] = (RATIO + 4.0) * modes[comp][1, 1, 1]
    return out


def paired(modes, forces):
    total = None
    for order in (1, 2, 3):
        part = None
        for comp in range(3):
            for key, force in forces[comp].items():
                if sum(key) == order:
                    term = modes[comp][key] * force
                    part = term if part is None else part + term
        part = CLASS[order] * part
        total = part if total is None else total + part
    return total


def pack_kernel(
    base_hbm, rhs_hbm, factor_hbm, ids_hbm, mask_hbm,
    up_ref, down_ref, res_ref, mod_ref, scale_ref, free_ref,
    base_ref, rhs_ref, factor_ref, ids_ref, mask_ref, sems,
):
    layers, height, width = factor_ref.shape
    pairs = (
        (base_hbm, base_ref),
        (ids_hbm, ids_ref),
        (factor_hbm, factor_ref),
        (mask_hbm, mask_ref),
        (rhs_hbm.at[0], rhs_ref),
    )
    copies = [pltpu.make_async_copy(source, target, sems.at[place]) for place, (source, target) in enumerate(pairs)]
    for copy in copies:
        copy.start()
    for copy in copies[:3]:
        copy.wait()
    ids = ids_ref[...]
    scale = jnp.full(ids.shape, base_ref[0])
    for zone in range(1, base_ref.shape[0]):
        scale = jnp.where(ids == zone, base_ref[zone], scale)
    modulus = factor_ref[...] * scale
    scale_ref[...] = scale
    mod_ref[...] = modulus
    copies[3].wait()
    free = 1.0 - mask_ref[...].astype(jnp.float32)
    free_ref[...] = free
    row = lax.broadcasted_iota(jnp.int32, (height, width), 0)

    def inverse(lower, upper, free):
        total = lower + upper
        total = total + last_lane(total)
        total = total + jnp.where(row == 0, 0.0, pltpu.roll(total, 1, 0))
        return free / (CORNER * total)

    top = inverse(modulus[layers - 2], modulus[layers - 1], free[layers - 1])
    second = top if layers == 2 else inverse(modulus[0], modulus[1], free[1])
    up_ref[3] = modulus[layers - 1]
    down_ref[6] = modulus[0]
    down_ref[7] = free[0]
    copies[4].wait()
    res = free[None] * rhs_ref[...]
    res_ref[...] = res
    up_ref[0:3] = res[:, layers - 1] * top
    down_ref[0:3] = res[:, 0]
    down_ref[3:6] = res[:, 1] * second


def image_kernel(free_ref, up_ref, down_ref, res_ref, mod_ref, z_ref, v_ref, sums_ref, carry, edge, inv):
    layers, height, width = mod_ref.shape
    blocks = height // ROWS

    def modulus(layer, rows):
        if layer < 0:
            return up_ref[3, rows, :]
        return mod_ref[layer, rows, :] if layer < layers else down_ref[6, rows, :]

    edge[:, 0:8, :] = jnp.zeros((layers + 1, 8, width), jnp.float32)
    carry[:, :, 0:8, :] = jnp.zeros((layers + 1, 3, 8, width), jnp.float32)
    z_ref[:, :, height : height + 8, :] = jnp.zeros((layers + 3, 3, 8, width), jnp.float32)
    v_ref[:, :, height : height + 8, :] = jnp.zeros((layers + 1, 3, 8, width), jnp.float32)

    def start_block(block, norm):
        start = pl.multiple_of(block * ROWS, ROWS)
        rows = pl.ds(start, ROWS)
        for plane in range(layers + 1):
            total = modulus(plane - 1, rows) + modulus(plane, rows)
            total = total + last_lane(total)
            edge[plane, pl.ds(start + 8, ROWS), :] = total
            total = total + edge[plane, pl.ds(start + 7, ROWS), :]
            free = down_ref[7, rows, :] if plane == layers else free_ref[plane, rows, :]
            inverse = free / (CORNER * total)
            inv[plane, rows, :] = inverse
            for comp in range(3):
                res = res_ref[comp, plane, rows, :] if plane < layers else down_ref[comp, rows, :]
                z = inverse * res
                z_ref[plane + 1, comp, rows, :] = z
                if plane < layers:
                    norm = norm + res * z
        for comp in range(3):
            z_ref[0, comp, rows, :] = up_ref[comp, rows, :]
            z_ref[layers + 2, comp, rows, :] = down_ref[3 + comp, rows, :]
        return norm

    zero = jnp.zeros((ROWS, width), jnp.float32)
    norm = lax.fori_loop(0, blocks, start_block, zero)

    def image_block(block, sums):
        along, across = sums
        start = pl.multiple_of(block * ROWS, ROWS)
        rows = pl.ds(start, ROWS)
        low = plane_modes(z_ref, 0, start)
        held = None
        for layer in range(layers + 2):
            high = plane_modes(z_ref, layer + 1, start)
            forces = stiff(layer_modes(low, high))
            stiffness = modulus(layer - 1, rows)
            weight = [None] + [CLASS[order] * stiffness for order in (1, 2, 3)]
            lower, upper = {}, {}
            for comp in range(3):
                for a in range(2):
                    for b in range(2):
                        change = weight[a + b + 1] * forces[comp][a, b, 1]
                        if a or b:
                            level = weight[a + b] * forces[comp][a, b, 0]
                            lower[comp, a, b] = level - change
                            upper[comp, a, b] = level + change
                        else:
                            lower[comp, a, b] = -change
                            upper[comp, a, b] = change
            if layer > 0:
                plane = layer - 1
                inverse = inv[plane, rows, :]
                for comp in range(3):
                    sides = []
                    for b in range(2):
                        level = held[comp, 0, b] + lower[comp, 0, b]
                        change = held[comp, 1, b] + lower[comp, 1, b]
                        sides.append(level - change + last_lane(level + change))
                    carry[plane, comp, pl.ds(start + 8, ROWS), :] = sides[0] + sides[1]
                    image = sides[0] - sides[1] + carry[plane, comp, pl.ds(start + 7, ROWS), :]
                    v = inverse * image
                    v_ref[plane, comp, rows, :] = v
                    if plane < layers:
                        along = along + image * z_ref[plane + 1, comp, rows, :]
                        across = across + image * v
            held = upper
            low = high
        return along, across

    along, across = lax.fori_loop(0, blocks, image_block, (zero, zero))

    def energy_block(block, energy):
        start = pl.multiple_of(block * ROWS, ROWS)
        low = plane_modes(v_ref, 0, start)
        for layer in range(layers):
            high = plane_modes(v_ref, layer + 1, start)
            modes = layer_modes(low, high)
            energy = energy + mod_ref[layer, pl.ds(start, ROWS), :] * paired(modes, stiff(modes))
            low = high
        return energy

    energy = lax.fori_loop(0, blocks, energy_block, zero)
    lane = lax.broadcasted_iota(jnp.int32, sums_ref.shape, 1)
    out = jnp.zeros(sums_ref.shape, jnp.float32)
    for place, part in enumerate((norm, along, across, energy)):
        out = jnp.where(lane == place, jnp.sum(part), out)
    sums_ref[...] = out


def term_kernel(load_ref, z_ref, v_ref, disp_ref, above_ref, scale_ref, term_ref, u_pad):
    layers, height, width = scale_ref.shape
    loads, share = term_ref.shape[0], term_ref.shape[3]
    u_pad[:, :, height : height + 8, :] = jnp.zeros((layers + 1, 3, 8, width), jnp.float32)
    for comp in range(3):
        for plane in range(layers + 1):
            u_pad[plane, comp, 0:height, :] = disp_ref[0, comp, plane] if plane < layers else above_ref[comp]

    def term_block(block, _):
        start = pl.multiple_of(block * ROWS, ROWS)
        rows = pl.ds(start, ROWS)
        place = lax.rem(start // share - load_ref[0] + loads, loads)
        target = pl.ds(pl.multiple_of(lax.rem(start, share), ROWS), ROWS)
        z_low = plane_modes(z_ref, 1, start)
        v_low = plane_modes(v_ref, 0, start)
        u_low = plane_modes(u_pad, 0, start)
        for layer in range(layers):
            z_high = plane_modes(z_ref, layer + 2, start)
            v_high = plane_modes(v_ref, layer + 1, start)
            u_high = plane_modes(u_pad, layer + 1, start)
            forces = stiff(layer_modes(u_low, u_high))
            scale = scale_ref[layer, rows, :]
            term_ref[place, 0, layer, target, :] = scale * paired(layer_modes(z_low, z_high), forces)
            term_ref[place, 1, layer, target, :] = scale * paired(layer_modes(v_low, v_high), forces)
            z_low, v_low, u_low = z_high, v_high, u_high
        return 0

    lax.fori_loop(0, height // ROWS, term_block, 0)


def finish_kernel(load_ref, sums_ref, z_ref, v_ref, *refs):
    x_ref, grad_ref = refs[-2:]
    term_refs = refs[:-2]
    loads, layers, height = len(term_refs), x_ref.shape[2], x_ref.shape[3]
    load = load_ref[0]
    device = lax.broadcasted_iota(jnp.int32, sums_ref.shape, 0)
    lane = lax.broadcasted_iota(jnp.int32, sums_ref.shape, 1)

    def weights(load):
        mine = jnp.where(lax.rem(device, loads) == load, sums_ref[...], 0.0)
        mine = jnp.sum(mine, axis=0, keepdims=True)
        norm, along, across, energy = [
            jnp.sum(jnp.where(lane[:1] == place, mine, 0.0), axis=1, keepdims=True) for place in range(4)
        ]
        first = norm / along
        later = first * first * across - norm
        second = later / (first * first * (energy - across * across / along))
        return first + second * (first * across / along), second * first

    for place in range(loads):
        from_z, from_v = weights(lax.rem(load - place + loads, loads))
        part = from_z * term_refs[place][0] - from_v * term_refs[place][1]
        total = part if place == 0 else total + part
        if place == 0:
            for comp in range(3):
                for plane in range(layers):
                    x_ref[0, comp, plane] = from_z * z_ref[plane + 1, comp, 0:height] - from_v * v_ref[plane, comp, 0:height]
    grad_ref[...] = total


def f32(*shape):
    return jax.ShapeDtypeStruct(shape, jnp.float32)


def shards(forward_disp, adjoint_rhs, modulus_factor, zone_base, zone_ids, fixed_mask):
    layers, height, width = modulus_factor.shape
    loads = lax.axis_size("load")
    devices = lax.axis_size("space") * loads
    load = lax.axis_index("load")
    whole = pl.BlockSpec(memory_space=pltpu.VMEM)
    scalar = pl.BlockSpec(memory_space=pltpu.SMEM)
    params = pltpu.CompilerParams(vmem_limit_bytes=12 * 2**20)
    pad = height + 8
    share = height // loads
    position = load.astype(jnp.int32)[None]

    up, down, res, modulus, scale, free = pl.pallas_call(
        pack_kernel,
        out_shape=(
            f32(4, height, width),
            f32(8, height, width),
            f32(3, layers, height, width),
            f32(layers, height, width),
            f32(layers, height, width),
            f32(layers, height, width),
        ),
        in_specs=[pl.BlockSpec(memory_space=pltpu.HBM)] * 5,
        out_specs=[whole] * 6,
        scratch_shapes=[
            pltpu.SMEM(zone_base.shape, jnp.float32),
            pltpu.VMEM((3, layers, height, width), jnp.float32),
            pltpu.VMEM((layers, height, width), jnp.float32),
            pltpu.VMEM((layers, height, width), jnp.int32),
            pltpu.VMEM((layers, height, width), jnp.int32),
            pltpu.SemaphoreType.DMA((5,)),
        ],
        compiler_params=pltpu.CompilerParams(vmem_limit_bytes=12 * 2**20),
        name="pack",
    )(*[pltpu.with_memory_space_constraint(part, pltpu.HBM) for part in (zone_base, adjoint_rhs, modulus_factor, zone_ids, fixed_mask)])
    from_below = permute(up, "space", 1)
    from_above = permute(down, "space", -1)
    lowest = forward_disp[0, :, 0]
    from_above, lowest = lax.optimization_barrier((from_above, lowest))
    above_disp = permute(lowest, "space", -1)
    z, v, sums = pl.pallas_call(
        image_kernel,
        out_shape=(
            f32(layers + 3, 3, pad, width),
            f32(layers + 1, 3, pad, width),
            f32(devices, 128),
        ),
        in_specs=[whole] * 5,
        out_specs=[whole] * 3,
        scratch_shapes=[
            pltpu.VMEM((layers + 1, 3, pad, width), jnp.float32),
            pltpu.VMEM((layers + 1, pad, width), jnp.float32),
            pltpu.VMEM((layers + 1, height, width), jnp.float32),
        ],
        compiler_params=params,
        name="image",
    )(free, from_below, from_above, res, modulus)
    sums = lax.all_to_all(sums, ("space", "load"), 0, 0, tiled=True)

    terms = pl.pallas_call(
        term_kernel,
        out_shape=f32(loads, 2, layers, share, width),
        in_specs=[scalar] + [whole] * 5,
        out_specs=whole,
        scratch_shapes=[pltpu.VMEM((layers + 1, 3, pad, width), jnp.float32)],
        compiler_params=params,
        cost_estimate=pl.CostEstimate(flops=4 * 10**9, bytes_accessed=8 * 2**20, transcendentals=0),
        name="term",
    )(position, z, v, forward_disp, above_disp, scale)
    sums, terms = lax.optimization_barrier((sums, terms))
    terms = [terms[0]] + [permute(terms[by], "load", by, wrap=True) for by in range(1, loads)]

    return pl.pallas_call(
        finish_kernel,
        out_shape=(f32(1, 3, layers, height, width), f32(layers, share, width)),
        in_specs=[scalar] + [whole] * (3 + loads),
        out_specs=[whole] * 2,
        compiler_params=params,
        name="finish",
    )(position, sums, z, v, *terms)


def solution(mesh):
    placed = (
        P("load", None, "space", None, None),
        P("load", None, "space", None, None),
        P("space", None, None),
        P(),
        P("space", None, None),
        P("space", None, None),
    )
    return jax.shard_map(
        shards,
        mesh=mesh,
        in_specs=placed,
        out_specs=(P("load", None, "space", None, None), P("space", "load", None)),
        check_vma=False,
    )
```

```python
import functools

import jax
import jax.numpy as jnp
from jax import lax
from jax.experimental import pallas as pl
from jax.experimental.pallas import tpu as pltpu
from jax.sharding import PartitionSpec as P

POISSON = 0.3
SHEAR = 0.5 / (1.0 + POISSON)
RATIO = 2.0 * POISSON / (1.0 - 2.0 * POISSON)
CLASS = [0.0] + [12.0 * SHEAR / 64.0 / 3.0**order for order in (1, 2, 3)]
CORNER = CLASS[1] * (RATIO + 4.0) + CLASS[2] * (2.0 * (RATIO + 3.0) + 2.0) + CLASS[3] * (RATIO + 4.0)
ROWS = 64


def permute(shard, axis, by, wrap=False):
    devices = lax.axis_size(axis)
    if wrap:
        pairs = [(i, (i + by) % devices) for i in range(devices)]
    else:
        pairs = [(i, i + by) for i in range(devices) if 0 <= i + by < devices]
    return lax.ppermute(shard, axis, pairs)


def next_lane(value):
    width = value.shape[-1]
    lane = lax.broadcasted_iota(jnp.int32, value.shape, value.ndim - 1)
    return jnp.where(lane == width - 1, 0.0, pltpu.roll(value, width - 1, value.ndim - 1))


def last_lane(value):
    lane = lax.broadcasted_iota(jnp.int32, value.shape, value.ndim - 1)
    return jnp.where(lane == 0, 0.0, pltpu.roll(value, 1, value.ndim - 1))


def plane_modes(ref, at, start, count):
    out = []
    for comp in range(3):
        here = ref[at + (comp, pl.ds(start, count))]
        below = ref[at + (comp, pl.ds(start + 1, count))]
        level, change = here + below, below - here
        level_next, change_next = next_lane(level), next_lane(change)
        out.append(((level + level_next, change + change_next), (level_next - level, change_next - change)))
    return out


def layer_modes(low, high):
    out = []
    for comp in range(3):
        modes = {}
        for a in range(2):
            for b in range(2):
                if a or b:
                    modes[a, b, 0] = low[comp][a][b] + high[comp][a][b]
                modes[a, b, 1] = high[comp][a][b] - low[comp][a][b]
        out.append(modes)
    return out


PAIRS = (((0, (1, 1, 0)), (2, (0, 1, 1))), ((1, (1, 1, 0)), (2, (1, 0, 1))), ((0, (1, 0, 1)), (1, (0, 1, 1))))


def stiff(modes):
    u, v, w = modes
    out = [{}, {}, {}]
    trace = RATIO * (u[1, 0, 0] + v[0, 1, 0] + w[0, 0, 1])
    out[0][1, 0, 0] = trace + 2.0 * u[1, 0, 0]
    out[1][0, 1, 0] = trace + 2.0 * v[0, 1, 0]
    out[2][0, 0, 1] = trace + 2.0 * w[0, 0, 1]
    for (one, at), (two, by) in PAIRS:
        both = RATIO * (modes[one][at] + modes[two][by])
        out[one][at] = both + 3.0 * modes[one][at]
        out[two][by] = both + 3.0 * modes[two][by]
    out[0][0, 1, 0] = out[1][1, 0, 0] = u[0, 1, 0] + v[1, 0, 0]
    out[1][0, 0, 1] = out[2][0, 1, 0] = v[0, 0, 1] + w[0, 1, 0]
    out[2][1, 0, 0] = out[0][0, 0, 1] = w[1, 0, 0] + u[0, 0, 1]
    first = u[0, 1, 1] + v[1, 0, 1]
    second = v[1, 0, 1] + w[1, 1, 0]
    third = w[1, 1, 0] + u[0, 1, 1]
    out[0][0, 1, 1] = first + third
    out[1][1, 0, 1] = first + second
    out[2][1, 1, 0] = second + third
    for comp in range(3):
        out[comp][1, 1, 1] = (RATIO + 4.0) * modes[comp][1, 1, 1]
    return out


def paired(modes, forces):
    total = None
    for order in (1, 2, 3):
        part = None
        for comp in range(3):
            for key, force in forces[comp].items():
                if sum(key) == order:
                    term = modes[comp][key] * force
                    part = term if part is None else part + term
        part = CLASS[order] * part
        total = part if total is None else total + part
    return total


def layer_forces(low, high, stiffness):
    forces = stiff(layer_modes(low, high))
    weight = [None] + [CLASS[order] * stiffness for order in (1, 2, 3)]
    lower, upper = {}, {}
    for comp in range(3):
        for a in range(2):
            for b in range(2):
                change = weight[a + b + 1] * forces[comp][a, b, 1]
                if a or b:
                    level = weight[a + b] * forces[comp][a, b, 0]
                    lower[comp, a, b] = level - change
                    upper[comp, a, b] = level + change
                else:
                    lower[comp, a, b] = -change
                    upper[comp, a, b] = change
    return lower, upper


def nodal(forces, comp, carry, start, count):
    sides = []
    for b in range(2):
        level, change = forces[comp, 0, b], forces[comp, 1, b]
        sides.append(level - change + last_lane(level + change))
    carry[comp, pl.ds(start + 8, count), :] = sides[0] + sides[1]
    return sides[0] - sides[1] + carry[comp, pl.ds(start + 7, count), :]


def add_up(parts):
    row = lax.broadcasted_iota(jnp.int32, (8, parts[0].shape[-1]), 0)
    out = jnp.zeros(row.shape, jnp.float32)
    for place, part in enumerate(parts):
        out = jnp.where(row == place, jnp.sum(part, axis=0, keepdims=True), out)
    return out


def inverse_diagonal(free, total, edge, start, count):
    total = total + last_lane(total)
    edge[pl.ds(start + 8, count), :] = total
    return free / (CORNER * (total + edge[pl.ds(start + 7, count), :]))


def pack_kernel(
    base_hbm, rhs_hbm, factor_hbm, ids_hbm, mask_hbm,
    up_ref, res_ref, mod_ref, scale_ref, free_ref,
    base_ref, rhs_ref, factor_ref, ids_ref, mask_ref, sems,
):
    layers, height, width = factor_ref.shape
    pairs = (
        (base_hbm, base_ref),
        (ids_hbm, ids_ref),
        (factor_hbm, factor_ref),
        (mask_hbm, mask_ref),
        (rhs_hbm.at[0], rhs_ref),
    )
    copies = [pltpu.make_async_copy(source, target, sems.at[place]) for place, (source, target) in enumerate(pairs)]
    for copy in copies:
        copy.start()
    for copy in copies[:3]:
        copy.wait()
    ids = ids_ref[...]
    scale = jnp.full(ids.shape, base_ref[0])
    for zone in range(1, base_ref.shape[0]):
        scale = jnp.where(ids == zone, base_ref[zone], scale)
    modulus = factor_ref[...] * scale
    scale_ref[...] = scale
    mod_ref[...] = modulus
    copies[3].wait()
    free = 1.0 - mask_ref[...].astype(jnp.float32)
    free_ref[...] = free
    row = lax.broadcasted_iota(jnp.int32, (height, width), 0)

    def inverse(lower, upper, free):
        total = lower + upper
        total = total + last_lane(total)
        total = total + jnp.where(row == 0, 0.0, pltpu.roll(total, 1, 0))
        return free / (CORNER * total)

    top = inverse(modulus[layers - 2], modulus[layers - 1], free[layers - 1])
    up_ref[3] = modulus[layers - 1]
    copies[4].wait()
    res = free[None] * rhs_ref[...]
    res_ref[...] = res
    up_ref[0:3] = res[:, layers - 1] * top


def down_kernel(rhs_hbm, disp_hbm, mod_ref, free_ref, down_ref, low_ref, edge, sems):
    copies = [
        pltpu.make_async_copy(rhs_hbm.at[0, :, 0], down_ref.at[0:3], sems.at[0]),
        pltpu.make_async_copy(rhs_hbm.at[0, :, 1], down_ref.at[3:6], sems.at[1]),
        pltpu.make_async_copy(disp_hbm.at[0, :, 0], low_ref, sems.at[2]),
    ]
    for copy in copies:
        copy.start()
    height = mod_ref.shape[1]
    down_ref[6] = mod_ref[0]
    down_ref[7] = free_ref[0]
    edge[0:8, :] = jnp.zeros((8, edge.shape[1]), jnp.float32)
    inverse = inverse_diagonal(free_ref[1], mod_ref[0] + mod_ref[1], edge, 0, height)
    for copy in copies:
        copy.wait()
    down_ref[3:6] = down_ref[3:6] * inverse


def below_kernel(up_ref, res_ref, mod_ref, free_ref, z_ref, v_ref, part_ref, inv_ref, sums_ref, under, carry, edge):
    layers, height, width = mod_ref.shape
    count = min(ROWS, height)
    edge[:, 0:8, :] = jnp.zeros((layers, 8, width), jnp.float32)
    carry[:, :, 0:8, :] = jnp.zeros((layers, 3, 8, width), jnp.float32)
    under[:, height : height + 8, :] = jnp.zeros((3, 8, width), jnp.float32)
    z_ref[:, :, height : height + 8, :] = jnp.zeros((layers, 3, 8, width), jnp.float32)
    v_ref[:, :, height : height + 8, :] = jnp.zeros((layers - 1, 3, 8, width), jnp.float32)
    zero = jnp.zeros((count, width), jnp.float32)

    def modulus(layer, rows):
        return mod_ref[layer, rows, :] if layer >= 0 else up_ref[3, rows, :]

    def start_block(block, norm):
        start = pl.multiple_of(block * count, count)
        rows = pl.ds(start, count)
        for plane in range(layers):
            total = modulus(plane - 1, rows) + modulus(plane, rows)
            inverse = inverse_diagonal(free_ref[plane, rows, :], total, edge.at[plane], start, count)
            inv_ref[plane, rows, :] = inverse
            for comp in range(3):
                res = res_ref[comp, plane, rows, :]
                z = inverse * res
                z_ref[plane, comp, rows, :] = z
                norm = norm + res * z
        for comp in range(3):
            under[comp, rows, :] = up_ref[comp, rows, :]
        return norm

    norm = lax.fori_loop(0, height // count, start_block, zero)

    def image_block(block, sums):
        along, across = sums
        start = pl.multiple_of(block * count, count)
        rows = pl.ds(start, count)
        low = plane_modes(under, (), start, count)
        held = None
        for layer in range(layers):
            high = plane_modes(z_ref, (layer,), start, count)
            lower, upper = layer_forces(low, high, modulus(layer - 1, rows))
            if layer > 0:
                plane = layer - 1
                lower = {key: lower[key] + held[key] for key in lower}
                for comp in range(3):
                    image = nodal(lower, comp, carry.at[plane], start, count)
                    v = inv_ref[plane, rows, :] * image
                    v_ref[plane, comp, rows, :] = v
                    along = along + image * z_ref[plane, comp, rows, :]
                    across = across + image * v
            held, low = upper, high
        for comp in range(3):
            part_ref[comp, rows, :] = nodal(held, comp, carry.at[layers - 1], start, count)
        return along, across

    along, across = lax.fori_loop(0, height // count, image_block, (zero, zero))
    sums_ref[...] = add_up((norm, along, across))


def above_kernel(
    down_ref, z_ref, low_v_ref, part_ref, inv_ref, mod_ref, low_sums_ref,
    top_ref, v_ref, sums_ref, over, carry, edge, inv,
):
    layers, height, width = mod_ref.shape
    count = min(ROWS, height)
    edge[0:8, :] = jnp.zeros((8, width), jnp.float32)
    carry[:, :, 0:8, :] = jnp.zeros((2, 3, 8, width), jnp.float32)
    over[:, height : height + 8, :] = jnp.zeros((3, 8, width), jnp.float32)
    top_ref[:, height : height + 8, :] = jnp.zeros((3, 8, width), jnp.float32)
    v_ref[:, :, height : height + 8, :] = jnp.zeros((2, 3, 8, width), jnp.float32)
    zero = jnp.zeros((count, width), jnp.float32)

    def start_block(block, _):
        start = pl.multiple_of(block * count, count)
        rows = pl.ds(start, count)
        total = mod_ref[layers - 1, rows, :] + down_ref[6, rows, :]
        inverse = inverse_diagonal(down_ref[7, rows, :], total, edge, start, count)
        inv[rows, :] = inverse
        for comp in range(3):
            top_ref[comp, rows, :] = inverse * down_ref[comp, rows, :]
            over[comp, rows, :] = down_ref[3 + comp, rows, :]
        return 0

    lax.fori_loop(0, height // count, start_block, 0)

    def image_block(block, sums):
        along, across = sums
        start = pl.multiple_of(block * count, count)
        rows = pl.ds(start, count)
        low = plane_modes(z_ref, (layers - 1,), start, count)
        high = plane_modes(top_ref, (), start, count)
        lower, held = layer_forces(low, high, mod_ref[layers - 1, rows, :])
        for comp in range(3):
            image = nodal(lower, comp, carry.at[0], start, count) + part_ref[comp, rows, :]
            v = inv_ref[layers - 1, rows, :] * image
            v_ref[0, comp, rows, :] = v
            along = along + image * z_ref[layers - 1, comp, rows, :]
            across = across + image * v
        lower, _ = layer_forces(high, plane_modes(over, (), start, count), down_ref[6, rows, :])
        lower = {key: lower[key] + held[key] for key in lower}
        for comp in range(3):
            v_ref[1, comp, rows, :] = inv[rows, :] * nodal(lower, comp, carry.at[1], start, count)
        return along, across

    along, across = lax.fori_loop(0, height // count, image_block, (zero, zero))

    def energy_block(block, energy):
        start = pl.multiple_of(block * count, count)
        low = None
        for plane in range(layers + 1):
            if plane < layers - 1:
                high = plane_modes(low_v_ref, (plane,), start, count)
            else:
                high = plane_modes(v_ref, (plane - layers + 1,), start, count)
            if plane > 0:
                modes = layer_modes(low, high)
                energy = energy + mod_ref[plane - 1, pl.ds(start, count), :] * paired(modes, stiff(modes))
            low = high
        return energy

    energy = lax.fori_loop(0, height // count, energy_block, zero)
    sums = low_sums_ref[...] + add_up((zero[:8], along, across, energy))
    sums = jnp.sum(sums, axis=1, keepdims=True)
    lane = lax.broadcasted_iota(jnp.int32, (8, width), 1)
    row = lax.broadcasted_iota(jnp.int32, (8, width), 0)
    sums = jnp.sum(jnp.where(lane == row, sums, 0.0), axis=0, keepdims=True)
    sums_ref[...] = jnp.broadcast_to(sums, sums_ref.shape)


def edge_modes(ref, at, block, count, last):
    out = []
    for comp in range(3):
        here = ref[at(comp) + (pl.ds(block * count, count),)]
        if last:
            row = lax.broadcasted_iota(jnp.int32, here.shape, 0)
            below = jnp.where(row == count - 1, 0.0, pltpu.roll(here, count - 1, 0))
        else:
            below = ref[at(comp) + (pl.ds(block * count + 1, count),)]
        level, change = here + below, below - here
        level_next, change_next = next_lane(level), next_lane(change)
        out.append(((level + level_next, change + change_next), (level_next - level, change_next - change)))
    return out


def term_kernel(load_ref, z_ref, top_ref, low_v_ref, v_ref, disp_ref, above_ref, scale_ref, term_ref):
    layers, height, width = scale_ref.shape
    loads, share = term_ref.shape[0], term_ref.shape[3]
    for block in range(loads):
        start = block * share
        place = lax.rem(block - load_ref[0] + loads, loads)
        low = None
        for plane in range(layers + 1):
            if plane < layers:
                z = plane_modes(z_ref, (plane,), start, share)
                u = edge_modes(disp_ref, lambda comp: (0, comp, plane), block, share, block == loads - 1)
            else:
                z = plane_modes(top_ref, (), start, share)
                u = edge_modes(above_ref, lambda comp: (comp,), block, share, block == loads - 1)
            if plane < layers - 1:
                v = plane_modes(low_v_ref, (plane,), start, share)
            else:
                v = plane_modes(v_ref, (plane - layers + 1,), start, share)
            high = [z, v, u]
            if plane > 0:
                z, v, u = [layer_modes(one, two) for one, two in zip(low, high)]
                forces = stiff(u)
                scale = scale_ref[plane - 1, start : start + share, :]
                term_ref[place, 0, plane - 1] = scale * paired(z, forces)
                term_ref[place, 1, plane - 1] = scale * paired(v, forces)
            low = high


def solve_weights(sums_ref, load, loads):
    device = lax.broadcasted_iota(jnp.int32, sums_ref.shape, 0)
    lane = lax.broadcasted_iota(jnp.int32, (1, sums_ref.shape[1]), 1)
    mine = jnp.where(lax.rem(device, loads) == load, sums_ref[...], 0.0)
    mine = jnp.sum(mine, axis=0, keepdims=True)
    norm, along, across, energy = [
        jnp.sum(jnp.where(lane == place, mine, 0.0), axis=1, keepdims=True) for place in range(4)
    ]
    first = norm / along
    later = first * first * across - norm
    second = later / (first * first * (energy - across * across / along))
    return first + second * (first * across / along), second * first


def disp_kernel(loads, load_ref, sums_ref, z_ref, low_v_ref, v_ref, x_ref):
    layers, height = x_ref.shape[2], x_ref.shape[3]
    from_z, from_v = solve_weights(sums_ref, load_ref[0], loads)
    for comp in range(3):
        for plane in range(layers):
            v = low_v_ref[plane, comp, 0:height] if plane < layers - 1 else v_ref[0, comp, 0:height]
            x_ref[0, comp, plane] = from_z * z_ref[plane, comp, 0:height] - from_v * v


def grad_kernel(load_ref, sums_ref, *refs):
    term_refs, grad_ref = refs[:-1], refs[-1]
    loads = len(term_refs)
    total = None
    for place in range(loads):
        from_z, from_v = solve_weights(sums_ref, lax.rem(load_ref[0] - place + loads, loads), loads)
        part = from_z * term_refs[place][0] - from_v * term_refs[place][1]
        total = part if total is None else total + part
    grad_ref[...] = total


def f32(*shape):
    return jax.ShapeDtypeStruct(shape, jnp.float32)


def shards(forward_disp, adjoint_rhs, modulus_factor, zone_base, zone_ids, fixed_mask):
    layers, height, width = modulus_factor.shape
    loads = lax.axis_size("load")
    devices = lax.axis_size("space") * loads
    load = lax.axis_index("load")
    whole = pl.BlockSpec(memory_space=pltpu.VMEM)
    scalar = pl.BlockSpec(memory_space=pltpu.SMEM)
    params = pltpu.CompilerParams(vmem_limit_bytes=12 * 2**20)
    pad = height + 8
    share = height // loads
    position = load.astype(jnp.int32)[None]

    def hbm(*arrays):
        return [pltpu.with_memory_space_constraint(array, pltpu.HBM) for array in arrays]

    far = pl.BlockSpec(memory_space=pltpu.HBM)
    up, res, modulus, scale, free = pl.pallas_call(
        pack_kernel,
        out_shape=[f32(4, height, width), f32(3, layers, height, width)] + [f32(layers, height, width)] * 3,
        in_specs=[far] * 5,
        out_specs=[whole] * 5,
        scratch_shapes=[
            pltpu.SMEM(zone_base.shape, jnp.float32),
            pltpu.VMEM((3, layers, height, width), jnp.float32),
            pltpu.VMEM((layers, height, width), jnp.float32),
            pltpu.VMEM((layers, height, width), jnp.int32),
            pltpu.VMEM((layers, height, width), jnp.int32),
            pltpu.SemaphoreType.DMA((5,)),
        ],
        compiler_params=params,
        name="pack",
    )(*hbm(zone_base, adjoint_rhs, modulus_factor, zone_ids, fixed_mask))
    from_below = permute(up, "space", 1)
    down, lowest = pl.pallas_call(
        down_kernel,
        out_shape=(f32(8, height, width), f32(3, height, width)),
        in_specs=[far] * 2 + [whole] * 2,
        out_specs=[whole] * 2,
        scratch_shapes=[pltpu.VMEM((pad, width), jnp.float32), pltpu.SemaphoreType.DMA((3,))],
        compiler_params=params,
        name="down",
    )(*hbm(adjoint_rhs, forward_disp), modulus, free)
    from_above = permute(down, "space", -1)

    z, low_v, part, inverse, low_sums = pl.pallas_call(
        below_kernel,
        out_shape=(
            f32(layers, 3, pad, width),
            f32(layers - 1, 3, pad, width),
            f32(3, height, width),
            f32(layers, height, width),
            f32(8, width),
        ),
        in_specs=[whole] * 4,
        out_specs=[whole] * 5,
        scratch_shapes=[
            pltpu.VMEM((3, pad, width), jnp.float32),
            pltpu.VMEM((layers, 3, pad, width), jnp.float32),
            pltpu.VMEM((layers, pad, width), jnp.float32),
        ],
        compiler_params=params,
        cost_estimate=pl.CostEstimate(flops=9 * 10**9, bytes_accessed=2 * 2**20, transcendentals=0),
        name="below",
    )(from_below, res, modulus, free)
    lowest, low_sums = lax.optimization_barrier((lowest, low_sums))
    above_disp = permute(lowest, "space", -1)

    top, v, sums = pl.pallas_call(
        above_kernel,
        out_shape=(f32(3, pad, width), f32(2, 3, pad, width), f32(devices, 128)),
        in_specs=[whole] * 7,
        out_specs=[whole] * 3,
        scratch_shapes=[
            pltpu.VMEM((3, pad, width), jnp.float32),
            pltpu.VMEM((2, 3, pad, width), jnp.float32),
            pltpu.VMEM((pad, width), jnp.float32),
            pltpu.VMEM((height, width), jnp.float32),
        ],
        compiler_params=params,
        name="above",
    )(from_above, z, low_v, part, inverse, modulus, low_sums)
    sums = lax.all_to_all(sums, ("space", "load"), 0, 0, tiled=True)

    terms = pl.pallas_call(
        term_kernel,
        out_shape=f32(loads, 2, layers, share, width),
        in_specs=[scalar] + [whole] * 7,
        out_specs=whole,
        compiler_params=params,
        name="term",
    )(position, z, top, low_v, v, forward_disp, above_disp, scale)
    sums, terms = lax.optimization_barrier((sums, terms))
    terms = [terms[0]] + [permute(terms[by], "load", by, wrap=True) for by in range(1, loads)]

    x = pl.pallas_call(
        functools.partial(disp_kernel, loads),
        out_shape=f32(1, 3, layers, height, width),
        in_specs=[scalar] + [whole] * 4,
        out_specs=whole,
        compiler_params=params,
        name="disp",
    )(position, sums, z, low_v, v)
    grad = pl.pallas_call(
        grad_kernel,
        out_shape=f32(layers, share, width),
        in_specs=[scalar] + [whole] * (1 + loads),
        out_specs=whole,
        compiler_params=params,
        name="grad",
    )(position, sums, *terms)
    return x, grad


def solution(mesh):
    placed = (
        P("load", None, "space", None, None),
        P("load", None, "space", None, None),
        P("space", None, None),
        P(),
        P("space", None, None),
        P("space", None, None),
    )
    return jax.shard_map(
        shards,
        mesh=mesh,
        in_specs=placed,
        out_specs=(P("load", None, "space", None, None), P("space", "load", None)),
        check_vma=False,
    )
```

```python
import functools

import jax
import jax.numpy as jnp
from jax import lax
from jax.experimental import pallas as pl
from jax.experimental.pallas import tpu as pltpu
from jax.sharding import PartitionSpec as P

POISSON = 0.3
SHEAR = 0.5 / (1.0 + POISSON)
RATIO = 2.0 * POISSON / (1.0 - 2.0 * POISSON)
CLASS = [0.0] + [12.0 * SHEAR / 64.0 / 3.0**order for order in (1, 2, 3)]
CORNER = CLASS[1] * (RATIO + 4.0) + CLASS[2] * (2.0 * (RATIO + 3.0) + 2.0) + CLASS[3] * (RATIO + 4.0)
ROWS = 64


def permute(shard, axis, by, wrap=False):
    devices = lax.axis_size(axis)
    if wrap:
        pairs = [(i, (i + by) % devices) for i in range(devices)]
    else:
        pairs = [(i, i + by) for i in range(devices) if 0 <= i + by < devices]
    return lax.ppermute(shard, axis, pairs)


def next_lane(value):
    width = value.shape[-1]
    lane = lax.broadcasted_iota(jnp.int32, value.shape, value.ndim - 1)
    return jnp.where(lane == width - 1, 0.0, pltpu.roll(value, width - 1, value.ndim - 1))


def last_lane(value):
    lane = lax.broadcasted_iota(jnp.int32, value.shape, value.ndim - 1)
    return jnp.where(lane == 0, 0.0, pltpu.roll(value, 1, value.ndim - 1))


def plane_modes(ref, at, start, count):
    out = []
    for comp in range(3):
        here = ref[at + (comp, pl.ds(start, count))]
        below = ref[at + (comp, pl.ds(start + 1, count))]
        level, change = here + below, below - here
        level_next, change_next = next_lane(level), next_lane(change)
        out.append(((level + level_next, change + change_next), (level_next - level, change_next - change)))
    return out


def layer_modes(low, high):
    out = []
    for comp in range(3):
        modes = {}
        for a in range(2):
            for b in range(2):
                if a or b:
                    modes[a, b, 0] = low[comp][a][b] + high[comp][a][b]
                modes[a, b, 1] = high[comp][a][b] - low[comp][a][b]
        out.append(modes)
    return out


PAIRS = (((0, (1, 1, 0)), (2, (0, 1, 1))), ((1, (1, 1, 0)), (2, (1, 0, 1))), ((0, (1, 0, 1)), (1, (0, 1, 1))))


def stiff(modes):
    u, v, w = modes
    out = [{}, {}, {}]
    trace = RATIO * (u[1, 0, 0] + v[0, 1, 0] + w[0, 0, 1])
    out[0][1, 0, 0] = trace + 2.0 * u[1, 0, 0]
    out[1][0, 1, 0] = trace + 2.0 * v[0, 1, 0]
    out[2][0, 0, 1] = trace + 2.0 * w[0, 0, 1]
    for (one, at), (two, by) in PAIRS:
        both = RATIO * (modes[one][at] + modes[two][by])
        out[one][at] = both + 3.0 * modes[one][at]
        out[two][by] = both + 3.0 * modes[two][by]
    out[0][0, 1, 0] = out[1][1, 0, 0] = u[0, 1, 0] + v[1, 0, 0]
    out[1][0, 0, 1] = out[2][0, 1, 0] = v[0, 0, 1] + w[0, 1, 0]
    out[2][1, 0, 0] = out[0][0, 0, 1] = w[1, 0, 0] + u[0, 0, 1]
    first = u[0, 1, 1] + v[1, 0, 1]
    second = v[1, 0, 1] + w[1, 1, 0]
    third = w[1, 1, 0] + u[0, 1, 1]
    out[0][0, 1, 1] = first + third
    out[1][1, 0, 1] = first + second
    out[2][1, 1, 0] = second + third
    for comp in range(3):
        out[comp][1, 1, 1] = (RATIO + 4.0) * modes[comp][1, 1, 1]
    return out


def paired(modes, forces):
    total = None
    for order in (1, 2, 3):
        part = None
        for comp in range(3):
            for key, force in forces[comp].items():
                if sum(key) == order:
                    term = modes[comp][key] * force
                    part = term if part is None else part + term
        part = CLASS[order] * part
        total = part if total is None else total + part
    return total


def layer_forces(low, high, stiffness):
    forces = stiff(layer_modes(low, high))
    weight = [None] + [CLASS[order] * stiffness for order in (1, 2, 3)]
    lower, upper = {}, {}
    for comp in range(3):
        for a in range(2):
            for b in range(2):
                change = weight[a + b + 1] * forces[comp][a, b, 1]
                if a or b:
                    level = weight[a + b] * forces[comp][a, b, 0]
                    lower[comp, a, b] = level - change
                    upper[comp, a, b] = level + change
                else:
                    lower[comp, a, b] = -change
                    upper[comp, a, b] = change
    return lower, upper


def nodal(forces, comp, carry, start, count):
    sides = []
    for b in range(2):
        level, change = forces[comp, 0, b], forces[comp, 1, b]
        sides.append(level - change + last_lane(level + change))
    carry[comp, pl.ds(start + 8, count), :] = sides[0] + sides[1]
    return sides[0] - sides[1] + carry[comp, pl.ds(start + 7, count), :]


def add_up(parts):
    row = lax.broadcasted_iota(jnp.int32, (8, parts[0].shape[-1]), 0)
    out = jnp.zeros(row.shape, jnp.float32)
    for place, part in enumerate(parts):
        out = jnp.where(row == place, jnp.sum(part, axis=0, keepdims=True), out)
    return out


def inverse_diagonal(free, total, edge, start, count):
    total = total + last_lane(total)
    edge[pl.ds(start + 8, count), :] = total
    return free / (CORNER * (total + edge[pl.ds(start + 7, count), :]))


def received(shared, item, load, start, count):
    loads, share = len(shared), shared[0].shape[0] // 3
    rows = pl.ds(pl.multiple_of(item * share + lax.rem(start, share), 8), count)
    distance = lax.rem(load - start // share + loads, loads)
    out = shared[0][rows, :]
    for by in range(1, loads):
        out = jnp.where(distance == by, shared[by][rows, :], out)
    return out


def pack_kernel(
    load_ref, base_hbm, rhs_hbm, factor_hbm, ids_hbm, mask_hbm, disp_hbm,
    up_ref, part_ref, down_ref, low_ref, res_ref, mod_ref, scale_ref, free_ref,
    base_ref, rhs_ref, factor_ref, ids_ref, mask_ref, edge, sems,
):
    layers, height, width = factor_ref.shape
    share = part_ref.shape[0] // 2
    mine = pl.ds(pl.multiple_of(load_ref[0] * share, 8), share)
    pairs = (
        (base_hbm, base_ref),
        (ids_hbm, ids_ref),
        (factor_hbm, factor_ref),
        (mask_hbm, mask_ref),
        (rhs_hbm.at[0], rhs_ref),
        (disp_hbm.at[0, :, 0], low_ref),
    )
    copies = [pltpu.make_async_copy(source, target, sems.at[place]) for place, (source, target) in enumerate(pairs)]
    for copy in copies:
        copy.start()
    edge[:, 0:8, :] = jnp.zeros((2, 8, width), jnp.float32)
    for copy in copies[:3]:
        copy.wait()
    scale = jnp.full(ids_ref.shape, base_ref[0])
    for zone in range(1, base_ref.shape[0]):
        scale = jnp.where(ids_ref[...] == zone, base_ref[zone], scale)
    modulus = factor_ref[...] * scale
    scale_ref[...] = scale
    mod_ref[...] = modulus
    copies[3].wait()
    free = 1.0 - mask_ref[...].astype(jnp.float32)
    free_ref[...] = free
    up_ref[3 * height :] = mod_ref[layers - 1, mine, :]
    part_ref[0:share] = mod_ref[0, mine, :]
    part_ref[share:] = free_ref[0, mine, :]
    top = inverse_diagonal(free[layers - 1], modulus[layers - 2] + modulus[layers - 1], edge.at[0], 0, height)
    second = top
    if layers > 2:
        second = inverse_diagonal(free[1], modulus[0] + modulus[1], edge.at[1], 0, height)
    copies[4].wait()
    for comp in range(3):
        res = free * rhs_ref[comp]
        res_ref[comp] = res
        up_ref[comp * height : (comp + 1) * height] = res[layers - 1] * top
        down_ref[comp] = res[0]
        down_ref[3 + comp] = res[1] * second
    copies[5].wait()


def below_kernel(load_ref, up_ref, res_ref, mod_ref, free_ref, *refs):
    z_ref, v_ref, part_ref, inv_ref, sums_ref, under, carry, edge = refs[-8:]
    shared = refs[:-8]
    layers, height, width = mod_ref.shape
    count = min(ROWS, height // len(shared))
    edge[:, 0:8, :] = jnp.zeros((layers, 8, width), jnp.float32)
    carry[:, :, 0:8, :] = jnp.zeros((layers, 3, 8, width), jnp.float32)
    under[:, height : height + 8, :] = jnp.zeros((3, 8, width), jnp.float32)
    z_ref[:, :, height : height + 8, :] = jnp.zeros((layers, 3, 8, width), jnp.float32)
    v_ref[:, :, height : height + 8, :] = jnp.zeros((layers - 1, 3, 8, width), jnp.float32)
    zero = jnp.zeros((count, width), jnp.float32)

    def modulus(layer, start):
        if layer < 0:
            return received(shared, 0, load_ref[0], start, count)
        return mod_ref[layer, pl.ds(start, count), :]

    def start_block(block, norm):
        start = pl.multiple_of(block * count, count)
        rows = pl.ds(start, count)
        for plane in range(layers):
            total = modulus(plane - 1, start) + modulus(plane, start)
            inverse = inverse_diagonal(free_ref[plane, rows, :], total, edge.at[plane], start, count)
            inv_ref[plane, rows, :] = inverse
            for comp in range(3):
                res = res_ref[comp, plane, rows, :]
                z = inverse * res
                z_ref[plane, comp, rows, :] = z
                norm = norm + res * z
        for comp in range(3):
            under[comp, rows, :] = up_ref[pl.ds(comp * height + start, count), :]
        return norm

    norm = lax.fori_loop(0, height // count, start_block, zero)

    def image_block(block, sums):
        along, across = sums
        start = pl.multiple_of(block * count, count)
        rows = pl.ds(start, count)
        low = plane_modes(under, (), start, count)
        held = None
        for layer in range(layers):
            high = plane_modes(z_ref, (layer,), start, count)
            lower, upper = layer_forces(low, high, modulus(layer - 1, start))
            if layer > 0:
                plane = layer - 1
                lower = {key: lower[key] + held[key] for key in lower}
                for comp in range(3):
                    image = nodal(lower, comp, carry.at[plane], start, count)
                    v = inv_ref[plane, rows, :] * image
                    v_ref[plane, comp, rows, :] = v
                    along = along + image * z_ref[plane, comp, rows, :]
                    across = across + image * v
            held, low = upper, high
        for comp in range(3):
            part_ref[comp, rows, :] = nodal(held, comp, carry.at[layers - 1], start, count)
        return along, across

    along, across = lax.fori_loop(0, height // count, image_block, (zero, zero))
    sums_ref[...] = add_up((norm, along, across))


def above_kernel(load_ref, down_ref, z_ref, low_v_ref, part_ref, inv_ref, mod_ref, low_sums_ref, *refs):
    top_ref, v_ref, sums_ref, over, carry, edge, inv = refs[-7:]
    shared = refs[:-7]
    layers, height, width = mod_ref.shape
    count = min(ROWS, height // len(shared))
    edge[0:8, :] = jnp.zeros((8, width), jnp.float32)
    carry[:, :, 0:8, :] = jnp.zeros((2, 3, 8, width), jnp.float32)
    over[:, height : height + 8, :] = jnp.zeros((3, 8, width), jnp.float32)
    top_ref[:, height : height + 8, :] = jnp.zeros((3, 8, width), jnp.float32)
    v_ref[:, :, height : height + 8, :] = jnp.zeros((2, 3, 8, width), jnp.float32)
    zero = jnp.zeros((count, width), jnp.float32)

    def start_block(block, _):
        start = pl.multiple_of(block * count, count)
        rows = pl.ds(start, count)
        total = mod_ref[layers - 1, rows, :] + received(shared, 1, load_ref[0], start, count)
        inverse = inverse_diagonal(received(shared, 2, load_ref[0], start, count), total, edge, start, count)
        inv[rows, :] = inverse
        for comp in range(3):
            top_ref[comp, rows, :] = inverse * down_ref[comp, rows, :]
            over[comp, rows, :] = down_ref[3 + comp, rows, :]
        return 0

    lax.fori_loop(0, height // count, start_block, 0)

    def image_block(block, sums):
        along, across = sums
        start = pl.multiple_of(block * count, count)
        rows = pl.ds(start, count)
        low = plane_modes(z_ref, (layers - 1,), start, count)
        high = plane_modes(top_ref, (), start, count)
        lower, held = layer_forces(low, high, mod_ref[layers - 1, rows, :])
        for comp in range(3):
            image = nodal(lower, comp, carry.at[0], start, count) + part_ref[comp, rows, :]
            v = inv_ref[layers - 1, rows, :] * image
            v_ref[0, comp, rows, :] = v
            along = along + image * z_ref[layers - 1, comp, rows, :]
            across = across + image * v
        stiffness = received(shared, 1, load_ref[0], start, count)
        lower, _ = layer_forces(high, plane_modes(over, (), start, count), stiffness)
        lower = {key: lower[key] + held[key] for key in lower}
        for comp in range(3):
            v_ref[1, comp, rows, :] = inv[rows, :] * nodal(lower, comp, carry.at[1], start, count)
        return along, across

    along, across = lax.fori_loop(0, height // count, image_block, (zero, zero))

    def energy_block(block, energy):
        start = pl.multiple_of(block * count, count)
        low = None
        for plane in range(layers + 1):
            if plane < layers - 1:
                high = plane_modes(low_v_ref, (plane,), start, count)
            else:
                high = plane_modes(v_ref, (plane - layers + 1,), start, count)
            if plane > 0:
                modes = layer_modes(low, high)
                energy = energy + mod_ref[plane - 1, pl.ds(start, count), :] * paired(modes, stiff(modes))
            low = high
        return energy

    energy = lax.fori_loop(0, height // count, energy_block, zero)
    sums = low_sums_ref[...] + add_up((zero[:8], along, across, energy))
    sums = jnp.sum(sums, axis=1, keepdims=True)
    lane = lax.broadcasted_iota(jnp.int32, (8, width), 1)
    row = lax.broadcasted_iota(jnp.int32, (8, width), 0)
    sums = jnp.sum(jnp.where(lane == row, sums, 0.0), axis=0, keepdims=True)
    sums_ref[...] = jnp.broadcast_to(sums, sums_ref.shape)


def edge_modes(ref, at, block, count, last):
    out = []
    for comp in range(3):
        here = ref[at(comp) + (pl.ds(block * count, count),)]
        if last:
            row = lax.broadcasted_iota(jnp.int32, here.shape, 0)
            below = jnp.where(row == count - 1, 0.0, pltpu.roll(here, count - 1, 0))
        else:
            below = ref[at(comp) + (pl.ds(block * count + 1, count),)]
        level, change = here + below, below - here
        level_next, change_next = next_lane(level), next_lane(change)
        out.append(((level + level_next, change + change_next), (level_next - level, change_next - change)))
    return out


def term_kernel(load_ref, z_ref, top_ref, low_v_ref, v_ref, disp_ref, above_ref, scale_ref, term_ref):
    layers, height, width = scale_ref.shape
    loads, share = term_ref.shape[0], term_ref.shape[3]
    for block in range(loads):
        start = block * share
        place = lax.rem(block - load_ref[0] + loads, loads)
        low = None
        for plane in range(layers + 1):
            if plane < layers:
                z = plane_modes(z_ref, (plane,), start, share)
                u = edge_modes(disp_ref, lambda comp: (0, comp, plane), block, share, block == loads - 1)
            else:
                z = plane_modes(top_ref, (), start, share)
                u = edge_modes(above_ref, lambda comp: (comp,), block, share, block == loads - 1)
            if plane < layers - 1:
                v = plane_modes(low_v_ref, (plane,), start, share)
            else:
                v = plane_modes(v_ref, (plane - layers + 1,), start, share)
            high = [z, v, u]
            if plane > 0:
                z, v, u = [layer_modes(one, two) for one, two in zip(low, high)]
                forces = stiff(u)
                scale = scale_ref[plane - 1, start : start + share, :]
                term_ref[place, 0, plane - 1] = scale * paired(z, forces)
                term_ref[place, 1, plane - 1] = scale * paired(v, forces)
            low = high


def solve_weights(sums_ref, load, loads):
    device = lax.broadcasted_iota(jnp.int32, sums_ref.shape, 0)
    lane = lax.broadcasted_iota(jnp.int32, (1, sums_ref.shape[1]), 1)
    mine = jnp.where(lax.rem(device, loads) == load, sums_ref[...], 0.0)
    mine = jnp.sum(mine, axis=0, keepdims=True)
    norm, along, across, energy = [
        jnp.sum(jnp.where(lane == place, mine, 0.0), axis=1, keepdims=True) for place in range(4)
    ]
    first = norm / along
    later = first * first * across - norm
    second = later / (first * first * (energy - across * across / along))
    return first + second * (first * across / along), second * first


def disp_kernel(loads, load_ref, sums_ref, z_ref, low_v_ref, v_ref, x_ref):
    layers, height = x_ref.shape[2], x_ref.shape[3]
    from_z, from_v = solve_weights(sums_ref, load_ref[0], loads)
    for comp in range(3):
        for plane in range(layers):
            v = low_v_ref[plane, comp, 0:height] if plane < layers - 1 else v_ref[0, comp, 0:height]
            x_ref[0, comp, plane] = from_z * z_ref[plane, comp, 0:height] - from_v * v


def grad_kernel(load_ref, sums_ref, *refs):
    term_refs, grad_ref = refs[:-1], refs[-1]
    loads = len(term_refs)
    total = None
    for place in range(loads):
        from_z, from_v = solve_weights(sums_ref, lax.rem(load_ref[0] - place + loads, loads), loads)
        part = from_z * term_refs[place][0] - from_v * term_refs[place][1]
        total = part if total is None else total + part
    grad_ref[...] = total


def f32(*shape):
    return jax.ShapeDtypeStruct(shape, jnp.float32)


def shards(forward_disp, adjoint_rhs, modulus_factor, zone_base, zone_ids, fixed_mask):
    layers, height, width = modulus_factor.shape
    loads = lax.axis_size("load")
    devices = lax.axis_size("space") * loads
    load = lax.axis_index("load")
    whole = pl.BlockSpec(memory_space=pltpu.VMEM)
    scalar = pl.BlockSpec(memory_space=pltpu.SMEM)
    params = pltpu.CompilerParams(vmem_limit_bytes=12 * 2**20)
    pad = height + 8
    share = height // loads
    position = load.astype(jnp.int32)[None]

    def hbm(*arrays):
        return [pltpu.with_memory_space_constraint(array, pltpu.HBM) for array in arrays]

    far = pl.BlockSpec(memory_space=pltpu.HBM)
    up, part_down, down, lowest, res, modulus, scale, free = pl.pallas_call(
        pack_kernel,
        out_shape=[f32(3 * height + share, width), f32(2 * share, width), f32(6, height, width), f32(3, height, width)]
        + [f32(3, layers, height, width)]
        + [f32(layers, height, width)] * 3,
        in_specs=[scalar] + [far] * 6,
        out_specs=[whole] * 8,
        scratch_shapes=[
            pltpu.SMEM(zone_base.shape, jnp.float32),
            pltpu.VMEM((3, layers, height, width), jnp.float32),
            pltpu.VMEM((layers, height, width), jnp.float32),
            pltpu.VMEM((layers, height, width), jnp.int32),
            pltpu.VMEM((layers, height, width), jnp.int32),
            pltpu.VMEM((2, pad, width), jnp.float32),
            pltpu.SemaphoreType.DMA((6,)),
        ],
        compiler_params=params,
        name="pack",
    )(position, *hbm(zone_base, adjoint_rhs, modulus_factor, zone_ids, fixed_mask, forward_disp))
    from_below = permute(up, "space", 1)
    shared = jnp.concatenate([from_below[3 * height :], permute(part_down, "space", -1)])
    shared = [shared] + [permute(shared, "load", by, wrap=True) for by in range(1, loads)]
    from_above = permute(down, "space", -1)

    z, low_v, part, inverse, low_sums = pl.pallas_call(
        below_kernel,
        out_shape=(
            f32(layers, 3, pad, width),
            f32(layers - 1, 3, pad, width),
            f32(3, height, width),
            f32(layers, height, width),
            f32(8, width),
        ),
        in_specs=[scalar] + [whole] * (4 + loads),
        out_specs=[whole] * 5,
        scratch_shapes=[
            pltpu.VMEM((3, pad, width), jnp.float32),
            pltpu.VMEM((layers, 3, pad, width), jnp.float32),
            pltpu.VMEM((layers, pad, width), jnp.float32),
        ],
        compiler_params=params,
        cost_estimate=pl.CostEstimate(flops=10**9, bytes_accessed=2**10, transcendentals=0),
        name="below",
    )(position, from_below, res, modulus, free, *shared)
    lowest, low_sums = lax.optimization_barrier((lowest, low_sums))
    above_disp = permute(lowest, "space", -1)

    top, v, sums = pl.pallas_call(
        above_kernel,
        out_shape=(f32(3, pad, width), f32(2, 3, pad, width), f32(devices, 128)),
        in_specs=[scalar] + [whole] * (7 + loads),
        out_specs=[whole] * 3,
        scratch_shapes=[
            pltpu.VMEM((3, pad, width), jnp.float32),
            pltpu.VMEM((2, 3, pad, width), jnp.float32),
            pltpu.VMEM((pad, width), jnp.float32),
            pltpu.VMEM((height, width), jnp.float32),
        ],
        compiler_params=params,
        name="above",
    )(position, from_above, z, low_v, part, inverse, modulus, low_sums, *shared)
    sums = lax.all_to_all(sums, ("space", "load"), 0, 0, tiled=True)

    terms = pl.pallas_call(
        term_kernel,
        out_shape=f32(loads, 2, layers, share, width),
        in_specs=[scalar] + [whole] * 7,
        out_specs=whole,
        compiler_params=params,
        name="term",
    )(position, z, top, low_v, v, forward_disp, above_disp, scale)
    sums, terms = lax.optimization_barrier((sums, terms))
    terms = [terms[0]] + [permute(terms[by], "load", by, wrap=True) for by in range(1, loads)]

    x = pl.pallas_call(
        functools.partial(disp_kernel, loads),
        out_shape=f32(1, 3, layers, height, width),
        in_specs=[scalar] + [whole] * 4,
        out_specs=whole,
        compiler_params=params,
        name="disp",
    )(position, sums, z, low_v, v)
    grad = pl.pallas_call(
        grad_kernel,
        out_shape=f32(layers, share, width),
        in_specs=[scalar] + [whole] * (1 + loads),
        out_specs=whole,
        compiler_params=params,
        name="grad",
    )(position, sums, *terms)
    return x, grad


def solution(mesh):
    placed = (
        P("load", None, "space", None, None),
        P("load", None, "space", None, None),
        P("space", None, None),
        P(),
        P("space", None, None),
        P("space", None, None),
    )
    return jax.shard_map(
        shards,
        mesh=mesh,
        in_specs=placed,
        out_specs=(P("load", None, "space", None, None), P("space", "load", None)),
        check_vma=False,
    )
```

```python
import functools

import jax
import jax.numpy as jnp
from jax import lax
from jax.experimental import pallas as pl
from jax.experimental.pallas import tpu as pltpu
from jax.sharding import PartitionSpec as P

POISSON = 0.3
SHEAR = 0.5 / (1.0 + POISSON)
RATIO = 2.0 * POISSON / (1.0 - 2.0 * POISSON)
CLASS = [0.0] + [12.0 * SHEAR / 64.0 / 3.0**order for order in (1, 2, 3)]
CORNER = CLASS[1] * (RATIO + 4.0) + CLASS[2] * (2.0 * (RATIO + 3.0) + 2.0) + CLASS[3] * (RATIO + 4.0)
ROWS = 64


def permute(shard, axis, by, wrap=False):
    devices = lax.axis_size(axis)
    if wrap:
        pairs = [(i, (i + by) % devices) for i in range(devices)]
    else:
        pairs = [(i, i + by) for i in range(devices) if 0 <= i + by < devices]
    return lax.ppermute(shard, axis, pairs)


def next_lane(value):
    width = value.shape[-1]
    lane = lax.broadcasted_iota(jnp.int32, value.shape, value.ndim - 1)
    return jnp.where(lane == width - 1, 0.0, pltpu.roll(value, width - 1, value.ndim - 1))


def last_lane(value):
    lane = lax.broadcasted_iota(jnp.int32, value.shape, value.ndim - 1)
    return jnp.where(lane == 0, 0.0, pltpu.roll(value, 1, value.ndim - 1))


def plane_modes(ref, at, start, count):
    out = []
    for comp in range(3):
        here = ref[at + (comp, pl.ds(start, count))]
        below = ref[at + (comp, pl.ds(start + 1, count))]
        level, change = here + below, below - here
        level_next, change_next = next_lane(level), next_lane(change)
        out.append(((level + level_next, change + change_next), (level_next - level, change_next - change)))
    return out


def layer_modes(low, high):
    out = []
    for comp in range(3):
        modes = {}
        for a in range(2):
            for b in range(2):
                if a or b:
                    modes[a, b, 0] = low[comp][a][b] + high[comp][a][b]
                modes[a, b, 1] = high[comp][a][b] - low[comp][a][b]
        out.append(modes)
    return out


PAIRS = (((0, (1, 1, 0)), (2, (0, 1, 1))), ((1, (1, 1, 0)), (2, (1, 0, 1))), ((0, (1, 0, 1)), (1, (0, 1, 1))))


def stiff(modes):
    u, v, w = modes
    out = [{}, {}, {}]
    trace = RATIO * (u[1, 0, 0] + v[0, 1, 0] + w[0, 0, 1])
    out[0][1, 0, 0] = trace + 2.0 * u[1, 0, 0]
    out[1][0, 1, 0] = trace + 2.0 * v[0, 1, 0]
    out[2][0, 0, 1] = trace + 2.0 * w[0, 0, 1]
    for (one, at), (two, by) in PAIRS:
        both = RATIO * (modes[one][at] + modes[two][by])
        out[one][at] = both + 3.0 * modes[one][at]
        out[two][by] = both + 3.0 * modes[two][by]
    out[0][0, 1, 0] = out[1][1, 0, 0] = u[0, 1, 0] + v[1, 0, 0]
    out[1][0, 0, 1] = out[2][0, 1, 0] = v[0, 0, 1] + w[0, 1, 0]
    out[2][1, 0, 0] = out[0][0, 0, 1] = w[1, 0, 0] + u[0, 0, 1]
    first = u[0, 1, 1] + v[1, 0, 1]
    second = v[1, 0, 1] + w[1, 1, 0]
    third = w[1, 1, 0] + u[0, 1, 1]
    out[0][0, 1, 1] = first + third
    out[1][1, 0, 1] = first + second
    out[2][1, 1, 0] = second + third
    for comp in range(3):
        out[comp][1, 1, 1] = (RATIO + 4.0) * modes[comp][1, 1, 1]
    return out


def paired(modes, forces):
    total = None
    for order in (1, 2, 3):
        part = None
        for comp in range(3):
            for key, force in forces[comp].items():
                if sum(key) == order:
                    term = modes[comp][key] * force
                    part = term if part is None else part + term
        part = CLASS[order] * part
        total = part if total is None else total + part
    return total


def layer_forces(low, high, stiffness):
    forces = stiff(layer_modes(low, high))
    weight = [None] + [CLASS[order] * stiffness for order in (1, 2, 3)]
    lower, upper = {}, {}
    for comp in range(3):
        for a in range(2):
            for b in range(2):
                change = weight[a + b + 1] * forces[comp][a, b, 1]
                if a or b:
                    level = weight[a + b] * forces[comp][a, b, 0]
                    lower[comp, a, b] = level - change
                    upper[comp, a, b] = level + change
                else:
                    lower[comp, a, b] = -change
                    upper[comp, a, b] = change
    return lower, upper


def nodal(forces, comp, carry, start, count):
    sides = []
    for b in range(2):
        level, change = forces[comp, 0, b], forces[comp, 1, b]
        sides.append(level - change + last_lane(level + change))
    carry[comp, pl.ds(start + 8, count), :] = sides[0] + sides[1]
    return sides[0] - sides[1] + carry[comp, pl.ds(start + 7, count), :]


def add_up(parts):
    row = lax.broadcasted_iota(jnp.int32, (8, parts[0].shape[-1]), 0)
    out = jnp.zeros(row.shape, jnp.float32)
    for place, part in enumerate(parts):
        out = jnp.where(row == place, jnp.sum(part, axis=0, keepdims=True), out)
    return out


def inverse_diagonal(free, total, edge, start, count):
    total = total + last_lane(total)
    edge[pl.ds(start + 8, count), :] = total
    return free / (CORNER * (total + edge[pl.ds(start + 7, count), :]))


def received(shared, item, load, start, count):
    loads, share = len(shared), shared[0].shape[0] // 3
    rows = pl.ds(pl.multiple_of(item * share + lax.rem(start, share), 8), count)
    distance = lax.rem(load - start // share + loads, loads)
    out = shared[0][rows, :]
    for by in range(1, loads):
        out = jnp.where(distance == by, shared[by][rows, :], out)
    return out


def pack_kernel(
    load_ref, base_hbm, rhs_hbm, factor_hbm, ids_hbm, mask_hbm, disp_hbm,
    up_ref, part_ref, down_ref, low_ref, res_ref, mod_ref, scale_ref, free_ref,
    base_ref, rhs_ref, factor_ref, ids_ref, mask_ref, edge, sems,
):
    layers, height, width = factor_ref.shape
    share = part_ref.shape[0] // 2
    mine = pl.ds(pl.multiple_of(load_ref[0] * share, 8), share)
    pairs = (
        (base_hbm, base_ref),
        (ids_hbm, ids_ref),
        (factor_hbm, factor_ref),
        (mask_hbm, mask_ref),
        (rhs_hbm.at[0], rhs_ref),
        (disp_hbm.at[0, :, 0], low_ref),
    )
    copies = [pltpu.make_async_copy(source, target, sems.at[place]) for place, (source, target) in enumerate(pairs)]
    for copy in copies:
        copy.start()
    edge[:, 0:8, :] = jnp.zeros((2, 8, width), jnp.float32)
    for copy in copies[:3]:
        copy.wait()
    scale = jnp.full(ids_ref.shape, base_ref[0])
    for zone in range(1, base_ref.shape[0]):
        scale = jnp.where(ids_ref[...] == zone, base_ref[zone], scale)
    modulus = factor_ref[...] * scale
    scale_ref[...] = scale
    mod_ref[...] = modulus
    copies[3].wait()
    free = 1.0 - mask_ref[...].astype(jnp.float32)
    free_ref[...] = free
    up_ref[3 * height :] = mod_ref[layers - 1, mine, :]
    part_ref[0:share] = mod_ref[0, mine, :]
    part_ref[share:] = free_ref[0, mine, :]
    top = inverse_diagonal(free[layers - 1], modulus[layers - 2] + modulus[layers - 1], edge.at[0], 0, height)
    second = top
    if layers > 2:
        second = inverse_diagonal(free[1], modulus[0] + modulus[1], edge.at[1], 0, height)
    copies[4].wait()
    for comp in range(3):
        res = free * rhs_ref[comp]
        res_ref[comp] = res
        up_ref[comp * height : (comp + 1) * height] = res[layers - 1] * top
        down_ref[comp] = res[0]
        down_ref[3 + comp] = res[1] * second
    copies[5].wait()


def below_kernel(load_ref, up_ref, res_ref, mod_ref, free_ref, *refs):
    z_ref, v_ref, part_ref, inv_ref, sums_ref, under, carry, edge = refs[-8:]
    shared = refs[:-8]
    layers, height, width = mod_ref.shape
    count = min(ROWS, height // len(shared))
    edge[:, 0:8, :] = jnp.zeros((layers, 8, width), jnp.float32)
    carry[:, :, 0:8, :] = jnp.zeros((layers, 3, 8, width), jnp.float32)
    under[:, height : height + 8, :] = jnp.zeros((3, 8, width), jnp.float32)
    z_ref[:, :, height : height + 8, :] = jnp.zeros((layers, 3, 8, width), jnp.float32)
    v_ref[:, :, height : height + 8, :] = jnp.zeros((layers - 1, 3, 8, width), jnp.float32)
    zero = jnp.zeros((count, width), jnp.float32)

    def modulus(layer, start):
        if layer < 0:
            return received(shared, 0, load_ref[0], start, count)
        return mod_ref[layer, pl.ds(start, count), :]

    def start_block(block, norm):
        start = pl.multiple_of(block * count, count)
        rows = pl.ds(start, count)
        for plane in range(layers):
            total = modulus(plane - 1, start) + modulus(plane, start)
            inverse = inverse_diagonal(free_ref[plane, rows, :], total, edge.at[plane], start, count)
            inv_ref[plane, rows, :] = inverse
            for comp in range(3):
                res = res_ref[comp, plane, rows, :]
                z = inverse * res
                z_ref[plane, comp, rows, :] = z
                norm = norm + res * z
        for comp in range(3):
            under[comp, rows, :] = up_ref[pl.ds(comp * height + start, count), :]
        return norm

    norm = lax.fori_loop(0, height // count, start_block, zero)

    def image_block(block, sums):
        along, across = sums
        start = pl.multiple_of(block * count, count)
        rows = pl.ds(start, count)
        low = plane_modes(under, (), start, count)
        held = None
        for layer in range(layers):
            high = plane_modes(z_ref, (layer,), start, count)
            lower, upper = layer_forces(low, high, modulus(layer - 1, start))
            if layer > 0:
                plane = layer - 1
                lower = {key: lower[key] + held[key] for key in lower}
                for comp in range(3):
                    image = nodal(lower, comp, carry.at[plane], start, count)
                    v = inv_ref[plane, rows, :] * image
                    v_ref[plane, comp, rows, :] = v
                    along = along + image * z_ref[plane, comp, rows, :]
                    across = across + image * v
            held, low = upper, high
        for comp in range(3):
            part_ref[comp, rows, :] = nodal(held, comp, carry.at[layers - 1], start, count)
        return along, across

    along, across = lax.fori_loop(0, height // count, image_block, (zero, zero))
    sums_ref[...] = add_up((norm, along, across))


def above_kernel(load_ref, down_ref, z_ref, low_v_ref, part_ref, inv_ref, mod_ref, low_sums_ref, *refs):
    top_ref, v_ref, sums_ref, over, carry, edge, inv = refs[-7:]
    shared = refs[:-7]
    layers, height, width = mod_ref.shape
    count = min(ROWS, height // len(shared))
    edge[0:8, :] = jnp.zeros((8, width), jnp.float32)
    carry[:, :, 0:8, :] = jnp.zeros((2, 3, 8, width), jnp.float32)
    over[:, height : height + 8, :] = jnp.zeros((3, 8, width), jnp.float32)
    top_ref[:, height : height + 8, :] = jnp.zeros((3, 8, width), jnp.float32)
    v_ref[:, :, height : height + 8, :] = jnp.zeros((2, 3, 8, width), jnp.float32)
    zero = jnp.zeros((count, width), jnp.float32)

    def start_block(block, _):
        start = pl.multiple_of(block * count, count)
        rows = pl.ds(start, count)
        total = mod_ref[layers - 1, rows, :] + received(shared, 1, load_ref[0], start, count)
        inverse = inverse_diagonal(received(shared, 2, load_ref[0], start, count), total, edge, start, count)
        inv[rows, :] = inverse
        for comp in range(3):
            top_ref[comp, rows, :] = inverse * down_ref[comp, rows, :]
            over[comp, rows, :] = down_ref[3 + comp, rows, :]
        return 0

    lax.fori_loop(0, height // count, start_block, 0)

    def image_block(block, sums):
        along, across = sums
        start = pl.multiple_of(block * count, count)
        rows = pl.ds(start, count)
        low = plane_modes(z_ref, (layers - 1,), start, count)
        high = plane_modes(top_ref, (), start, count)
        lower, held = layer_forces(low, high, mod_ref[layers - 1, rows, :])
        for comp in range(3):
            image = nodal(lower, comp, carry.at[0], start, count) + part_ref[comp, rows, :]
            v = inv_ref[layers - 1, rows, :] * image
            v_ref[0, comp, rows, :] = v
            along = along + image * z_ref[layers - 1, comp, rows, :]
            across = across + image * v
        stiffness = received(shared, 1, load_ref[0], start, count)
        lower, _ = layer_forces(high, plane_modes(over, (), start, count), stiffness)
        lower = {key: lower[key] + held[key] for key in lower}
        for comp in range(3):
            v_ref[1, comp, rows, :] = inv[rows, :] * nodal(lower, comp, carry.at[1], start, count)
        return along, across

    along, across = lax.fori_loop(0, height // count, image_block, (zero, zero))

    def energy_block(block, energy):
        start = pl.multiple_of(block * count, count)
        low = None
        for plane in range(layers + 1):
            if plane < layers - 1:
                high = plane_modes(low_v_ref, (plane,), start, count)
            else:
                high = plane_modes(v_ref, (plane - layers + 1,), start, count)
            if plane > 0:
                modes = layer_modes(low, high)
                energy = energy + mod_ref[plane - 1, pl.ds(start, count), :] * paired(modes, stiff(modes))
            low = high
        return energy

    energy = lax.fori_loop(0, height // count, energy_block, zero)
    sums = low_sums_ref[...] + add_up((zero[:8], along, across, energy))
    sums = jnp.sum(sums, axis=1, keepdims=True)
    lane = lax.broadcasted_iota(jnp.int32, (8, width), 1)
    row = lax.broadcasted_iota(jnp.int32, (8, width), 0)
    sums = jnp.sum(jnp.where(lane == row, sums, 0.0), axis=0, keepdims=True)
    sums_ref[...] = jnp.broadcast_to(sums, sums_ref.shape)


def edge_modes(ref, at, block, count, last):
    out = []
    for comp in range(3):
        here = ref[at(comp) + (pl.ds(block * count, count),)]
        if last:
            row = lax.broadcasted_iota(jnp.int32, here.shape, 0)
            below = jnp.where(row == count - 1, 0.0, pltpu.roll(here, count - 1, 0))
        else:
            below = ref[at(comp) + (pl.ds(block * count + 1, count),)]
        level, change = here + below, below - here
        level_next, change_next = next_lane(level), next_lane(change)
        out.append(((level + level_next, change + change_next), (level_next - level, change_next - change)))
    return out


def early_kernel(z_ref, disp_ref, scale_ref, early_ref):
    layers, height, width = early_ref.shape
    count = min(ROWS, height)
    for block in range(height // count):
        start = block * count
        low = None
        for plane in range(layers + 1):
            last = block == height // count - 1
            u = edge_modes(disp_ref, lambda comp: (0, comp, plane), block, count, last)
            high = (plane_modes(z_ref, (plane,), start, count), u)
            if plane > 0:
                z, u = [layer_modes(one, two) for one, two in zip(low, high)]
                rows = slice(start, start + count)
                early_ref[plane - 1, rows, :] = scale_ref[plane - 1, rows, :] * paired(z, stiff(u))
            low = high


def term_kernel(
    load_ref, early_ref, z_ref, top_ref, low_v_ref, v_ref, disp_ref, above_ref, scale_ref, term_ref
):
    layers, height, width = scale_ref.shape
    loads, share = term_ref.shape[0], term_ref.shape[3]
    for block in range(loads):
        start = block * share
        place = lax.rem(block - load_ref[0] + loads, loads)
        low = None
        for plane in range(layers + 1):
            z = None
            if plane == layers - 1:
                z = plane_modes(z_ref, (plane,), start, share)
            if plane == layers:
                z = plane_modes(top_ref, (), start, share)
            if plane < layers:
                u = edge_modes(disp_ref, lambda comp: (0, comp, plane), block, share, block == loads - 1)
            else:
                u = edge_modes(above_ref, lambda comp: (comp,), block, share, block == loads - 1)
            if plane < layers - 1:
                v = plane_modes(low_v_ref, (plane,), start, share)
            else:
                v = plane_modes(v_ref, (plane - layers + 1,), start, share)
            high = [v, u, z]
            if plane > 0:
                layer = plane - 1
                scale = scale_ref[layer, start : start + share, :]
                v, u = [layer_modes(one, two) for one, two in zip(low[:2], high[:2])]
                forces = stiff(u)
                if plane < layers:
                    term_ref[place, 0, layer] = early_ref[layer, start : start + share, :]
                else:
                    term_ref[place, 0, layer] = scale * paired(layer_modes(low[2], z), forces)
                term_ref[place, 1, layer] = scale * paired(v, forces)
            low = high


def solve_weights(sums_ref, load, loads):
    device = lax.broadcasted_iota(jnp.int32, sums_ref.shape, 0)
    lane = lax.broadcasted_iota(jnp.int32, (1, sums_ref.shape[1]), 1)
    mine = jnp.where(lax.rem(device, loads) == load, sums_ref[...], 0.0)
    mine = jnp.sum(mine, axis=0, keepdims=True)
    norm, along, across, energy = [
        jnp.sum(jnp.where(lane == place, mine, 0.0), axis=1, keepdims=True) for place in range(4)
    ]
    first = norm / along
    later = first * first * across - norm
    second = later / (first * first * (energy - across * across / along))
    return first + second * (first * across / along), second * first


def disp_kernel(loads, load_ref, sums_ref, z_ref, low_v_ref, v_ref, x_ref, weight_ref):
    layers, height = x_ref.shape[2], x_ref.shape[3]
    for place in range(loads):
        weights = solve_weights(sums_ref, lax.rem(load_ref[0] - place + loads, loads), loads)
        for which, weight in enumerate(weights):
            weight_ref[2 * place + which] = jnp.broadcast_to(weight, weight_ref.shape[1:])
    from_z, from_v = weight_ref[0, 0:1, :], weight_ref[1, 0:1, :]
    for comp in range(3):
        for plane in range(layers):
            v = low_v_ref[plane, comp, 0:height] if plane < layers - 1 else v_ref[0, comp, 0:height]
            x_ref[0, comp, plane] = from_z * z_ref[plane, comp, 0:height] - from_v * v


def grad_kernel(weight_ref, *refs):
    term_refs, grad_ref = refs[:-1], refs[-1]
    total = None
    for place, term_ref in enumerate(term_refs):
        part = weight_ref[2 * place, 0:1, :] * term_ref[0] - weight_ref[2 * place + 1, 0:1, :] * term_ref[1]
        total = part if total is None else total + part
    grad_ref[...] = total


def f32(*shape):
    return jax.ShapeDtypeStruct(shape, jnp.float32)


def shards(forward_disp, adjoint_rhs, modulus_factor, zone_base, zone_ids, fixed_mask):
    layers, height, width = modulus_factor.shape
    loads = lax.axis_size("load")
    devices = lax.axis_size("space") * loads
    load = lax.axis_index("load")
    whole = pl.BlockSpec(memory_space=pltpu.VMEM)
    scalar = pl.BlockSpec(memory_space=pltpu.SMEM)
    params = pltpu.CompilerParams(vmem_limit_bytes=12 * 2**20)
    pad = height + 8
    share = height // loads
    position = load.astype(jnp.int32)[None]

    def hbm(*arrays):
        return [pltpu.with_memory_space_constraint(array, pltpu.HBM) for array in arrays]

    far = pl.BlockSpec(memory_space=pltpu.HBM)
    up, part_down, down, lowest, res, modulus, scale, free = pl.pallas_call(
        pack_kernel,
        out_shape=[f32(3 * height + share, width), f32(2 * share, width), f32(6, height, width), f32(3, height, width)]
        + [f32(3, layers, height, width)]
        + [f32(layers, height, width)] * 3,
        in_specs=[scalar] + [far] * 6,
        out_specs=[whole] * 8,
        scratch_shapes=[
            pltpu.SMEM(zone_base.shape, jnp.float32),
            pltpu.VMEM((3, layers, height, width), jnp.float32),
            pltpu.VMEM((layers, height, width), jnp.float32),
            pltpu.VMEM((layers, height, width), jnp.int32),
            pltpu.VMEM((layers, height, width), jnp.int32),
            pltpu.VMEM((2, pad, width), jnp.float32),
            pltpu.SemaphoreType.DMA((6,)),
        ],
        compiler_params=params,
        name="pack",
    )(position, *hbm(zone_base, adjoint_rhs, modulus_factor, zone_ids, fixed_mask, forward_disp))
    from_below = permute(up, "space", 1)
    shared = jnp.concatenate([from_below[3 * height :], permute(part_down, "space", -1)])
    shared = [shared] + [permute(shared, "load", by, wrap=True) for by in range(1, loads)]
    from_above = permute(down, "space", -1)

    z, low_v, part, inverse, low_sums = pl.pallas_call(
        below_kernel,
        out_shape=(
            f32(layers, 3, pad, width),
            f32(layers - 1, 3, pad, width),
            f32(3, height, width),
            f32(layers, height, width),
            f32(8, width),
        ),
        in_specs=[scalar] + [whole] * (4 + loads),
        out_specs=[whole] * 5,
        scratch_shapes=[
            pltpu.VMEM((3, pad, width), jnp.float32),
            pltpu.VMEM((layers, 3, pad, width), jnp.float32),
            pltpu.VMEM((layers, pad, width), jnp.float32),
        ],
        compiler_params=params,
        cost_estimate=pl.CostEstimate(flops=10**9, bytes_accessed=2**10, transcendentals=0),
        name="below",
    )(position, from_below, res, modulus, free, *shared)
    early = pl.pallas_call(
        early_kernel,
        out_shape=f32(layers - 1, height, width),
        in_specs=[whole] * 3,
        out_specs=whole,
        compiler_params=params,
        name="early",
    )(z, forward_disp, scale)
    lowest, early = lax.optimization_barrier((lowest, early))
    above_disp = permute(lowest, "space", -1)

    top, v, sums = pl.pallas_call(
        above_kernel,
        out_shape=(f32(3, pad, width), f32(2, 3, pad, width), f32(devices, 128)),
        in_specs=[scalar] + [whole] * (7 + loads),
        out_specs=[whole] * 3,
        scratch_shapes=[
            pltpu.VMEM((3, pad, width), jnp.float32),
            pltpu.VMEM((2, 3, pad, width), jnp.float32),
            pltpu.VMEM((pad, width), jnp.float32),
            pltpu.VMEM((height, width), jnp.float32),
        ],
        compiler_params=params,
        name="above",
    )(position, from_above, z, low_v, part, inverse, modulus, low_sums, *shared)
    sums = lax.all_to_all(sums, ("space", "load"), 0, 0, tiled=True)

    terms = pl.pallas_call(
        term_kernel,
        out_shape=f32(loads, 2, layers, share, width),
        in_specs=[scalar] + [whole] * 8,
        out_specs=whole,
        compiler_params=params,
        name="term",
    )(position, early, z, top, low_v, v, forward_disp, above_disp, scale)
    sums, terms = lax.optimization_barrier((sums, terms))
    terms = [terms[0]] + [permute(terms[by], "load", by, wrap=True) for by in range(1, loads)]

    x, weights = pl.pallas_call(
        functools.partial(disp_kernel, loads),
        out_shape=(f32(1, 3, layers, height, width), f32(2 * loads, 8, width)),
        in_specs=[scalar] + [whole] * 4,
        out_specs=[whole] * 2,
        compiler_params=params,
        name="disp",
    )(position, sums, z, low_v, v)
    grad = pl.pallas_call(
        grad_kernel,
        out_shape=f32(layers, share, width),
        in_specs=[whole] * (1 + loads),
        out_specs=whole,
        compiler_params=params,
        name="grad",
    )(weights, *terms)
    return x, grad


def solution(mesh):
    placed = (
        P("load", None, "space", None, None),
        P("load", None, "space", None, None),
        P("space", None, None),
        P(),
        P("space", None, None),
        P("space", None, None),
    )
    return jax.shard_map(
        shards,
        mesh=mesh,
        in_specs=placed,
        out_specs=(P("load", None, "space", None, None), P("space", "load", None)),
        check_vma=False,
    )
```

```python
import functools

import jax
import jax.numpy as jnp
from jax import lax
from jax.experimental import pallas as pl
from jax.experimental.pallas import tpu as pltpu
from jax.sharding import PartitionSpec as P

POISSON = 0.3
SHEAR = 0.5 / (1.0 + POISSON)
RATIO = 2.0 * POISSON / (1.0 - 2.0 * POISSON)
CLASS = [0.0] + [12.0 * SHEAR / 64.0 / 3.0**order for order in (1, 2, 3)]
CORNER = CLASS[1] * (RATIO + 4.0) + CLASS[2] * (2.0 * (RATIO + 3.0) + 2.0) + CLASS[3] * (RATIO + 4.0)
ROWS = 64


def permute(shard, axis, by, wrap=False):
    devices = lax.axis_size(axis)
    if wrap:
        pairs = [(i, (i + by) % devices) for i in range(devices)]
    else:
        pairs = [(i, i + by) for i in range(devices) if 0 <= i + by < devices]
    return lax.ppermute(shard, axis, pairs)


def next_lane(value):
    width = value.shape[-1]
    lane = lax.broadcasted_iota(jnp.int32, value.shape, value.ndim - 1)
    return jnp.where(lane == width - 1, 0.0, pltpu.roll(value, width - 1, value.ndim - 1))


def last_lane(value):
    lane = lax.broadcasted_iota(jnp.int32, value.shape, value.ndim - 1)
    return jnp.where(lane == 0, 0.0, pltpu.roll(value, 1, value.ndim - 1))


def plane_modes(ref, at, start, count):
    out = []
    for comp in range(3):
        here = ref[at + (comp, pl.ds(start, count))]
        below = ref[at + (comp, pl.ds(start + 1, count))]
        level, change = here + below, below - here
        level_next, change_next = next_lane(level), next_lane(change)
        out.append(((level + level_next, change + change_next), (level_next - level, change_next - change)))
    return out


def layer_modes(low, high):
    out = []
    for comp in range(3):
        modes = {}
        for a in range(2):
            for b in range(2):
                if a or b:
                    modes[a, b, 0] = low[comp][a][b] + high[comp][a][b]
                modes[a, b, 1] = high[comp][a][b] - low[comp][a][b]
        out.append(modes)
    return out


PAIRS = (((0, (1, 1, 0)), (2, (0, 1, 1))), ((1, (1, 1, 0)), (2, (1, 0, 1))), ((0, (1, 0, 1)), (1, (0, 1, 1))))


def stiff(modes):
    u, v, w = modes
    out = [{}, {}, {}]
    trace = RATIO * (u[1, 0, 0] + v[0, 1, 0] + w[0, 0, 1])
    out[0][1, 0, 0] = trace + 2.0 * u[1, 0, 0]
    out[1][0, 1, 0] = trace + 2.0 * v[0, 1, 0]
    out[2][0, 0, 1] = trace + 2.0 * w[0, 0, 1]
    for (one, at), (two, by) in PAIRS:
        both = RATIO * (modes[one][at] + modes[two][by])
        out[one][at] = both + 3.0 * modes[one][at]
        out[two][by] = both + 3.0 * modes[two][by]
    out[0][0, 1, 0] = out[1][1, 0, 0] = u[0, 1, 0] + v[1, 0, 0]
    out[1][0, 0, 1] = out[2][0, 1, 0] = v[0, 0, 1] + w[0, 1, 0]
    out[2][1, 0, 0] = out[0][0, 0, 1] = w[1, 0, 0] + u[0, 0, 1]
    first = u[0, 1, 1] + v[1, 0, 1]
    second = v[1, 0, 1] + w[1, 1, 0]
    third = w[1, 1, 0] + u[0, 1, 1]
    out[0][0, 1, 1] = first + third
    out[1][1, 0, 1] = first + second
    out[2][1, 1, 0] = second + third
    for comp in range(3):
        out[comp][1, 1, 1] = (RATIO + 4.0) * modes[comp][1, 1, 1]
    return out


def paired(modes, forces):
    total = None
    for order in (1, 2, 3):
        part = None
        for comp in range(3):
            for key, force in forces[comp].items():
                if sum(key) == order:
                    term = modes[comp][key] * force
                    part = term if part is None else part + term
        part = CLASS[order] * part
        total = part if total is None else total + part
    return total


def layer_forces(low, high, stiffness):
    forces = stiff(layer_modes(low, high))
    weight = [None] + [CLASS[order] * stiffness for order in (1, 2, 3)]
    lower, upper = {}, {}
    for comp in range(3):
        for a in range(2):
            for b in range(2):
                change = weight[a + b + 1] * forces[comp][a, b, 1]
                if a or b:
                    level = weight[a + b] * forces[comp][a, b, 0]
                    lower[comp, a, b] = level - change
                    upper[comp, a, b] = level + change
                else:
                    lower[comp, a, b] = -change
                    upper[comp, a, b] = change
    return lower, upper


def nodal(forces, comp, carry, start, count):
    sides = []
    for b in range(2):
        level, change = forces[comp, 0, b], forces[comp, 1, b]
        sides.append(level - change + last_lane(level + change))
    carry[comp, pl.ds(start + 8, count), :] = sides[0] + sides[1]
    return sides[0] - sides[1] + carry[comp, pl.ds(start + 7, count), :]


def add_up(parts):
    row = lax.broadcasted_iota(jnp.int32, (8, parts[0].shape[-1]), 0)
    out = jnp.zeros(row.shape, jnp.float32)
    for place, part in enumerate(parts):
        out = jnp.where(row == place, jnp.sum(part, axis=0, keepdims=True), out)
    return out


def inverse_diagonal(free, total, edge, start, count):
    total = total + last_lane(total)
    edge[pl.ds(start + 8, count), :] = total
    return free / (CORNER * (total + edge[pl.ds(start + 7, count), :]))


def received(shared, item, load, start, count):
    loads, share = len(shared), shared[0].shape[0] // 3
    rows = pl.ds(pl.multiple_of(item * share + lax.rem(start, share), 8), count)
    distance = lax.rem(load - start // share + loads, loads)
    out = shared[0][rows, :]
    for by in range(1, loads):
        out = jnp.where(distance == by, shared[by][rows, :], out)
    return out


def pack_kernel(
    load_ref, base_hbm, rhs_hbm, factor_hbm, ids_hbm, mask_hbm, disp_hbm,
    up_ref, part_ref, down_ref, low_ref, res_ref, mod_ref, scale_ref, free_ref,
    base_ref, rhs_ref, factor_ref, ids_ref, mask_ref, edge, sems,
):
    layers, height, width = factor_ref.shape
    share = part_ref.shape[0] // 2
    mine = pl.ds(pl.multiple_of(load_ref[0] * share, 8), share)
    pairs = (
        (base_hbm, base_ref),
        (ids_hbm, ids_ref),
        (factor_hbm, factor_ref),
        (mask_hbm, mask_ref),
        (rhs_hbm.at[0], rhs_ref),
        (disp_hbm.at[0, :, 0], low_ref),
    )
    copies = [pltpu.make_async_copy(source, target, sems.at[place]) for place, (source, target) in enumerate(pairs)]
    for copy in copies:
        copy.start()
    edge[:, 0:8, :] = jnp.zeros((2, 8, width), jnp.float32)
    for copy in copies[:3]:
        copy.wait()
    scale = jnp.full(ids_ref.shape, base_ref[0])
    for zone in range(1, base_ref.shape[0]):
        scale = jnp.where(ids_ref[...] == zone, base_ref[zone], scale)
    modulus = factor_ref[...] * scale
    scale_ref[...] = scale
    mod_ref[...] = modulus
    copies[3].wait()
    free = 1.0 - mask_ref[...].astype(jnp.float32)
    free_ref[...] = free
    up_ref[3 * height :] = mod_ref[layers - 1, mine, :]
    part_ref[0:share] = mod_ref[0, mine, :]
    part_ref[share:] = free_ref[0, mine, :]
    top = inverse_diagonal(free[layers - 1], modulus[layers - 2] + modulus[layers - 1], edge.at[0], 0, height)
    second = top
    if layers > 2:
        second = inverse_diagonal(free[1], modulus[0] + modulus[1], edge.at[1], 0, height)
    copies[4].wait()
    for comp in range(3):
        res = free * rhs_ref[comp]
        res_ref[comp] = res
        up_ref[comp * height : (comp + 1) * height] = res[layers - 1] * top
        down_ref[comp] = res[0]
        down_ref[3 + comp] = res[1] * second
    copies[5].wait()


def below_kernel(load_ref, up_ref, res_ref, mod_ref, free_ref, *refs):
    z_ref, v_ref, part_ref, inv_ref, sums_ref, under, carry, edge = refs[-8:]
    shared = refs[:-8]
    layers, height, width = mod_ref.shape
    count = min(ROWS, height // len(shared))
    edge[:, 0:8, :] = jnp.zeros((layers, 8, width), jnp.float32)
    carry[:, :, 0:8, :] = jnp.zeros((layers, 3, 8, width), jnp.float32)
    under[:, height : height + 8, :] = jnp.zeros((3, 8, width), jnp.float32)
    z_ref[:, :, height : height + 8, :] = jnp.zeros((layers, 3, 8, width), jnp.float32)
    v_ref[:, :, height : height + 8, :] = jnp.zeros((layers - 1, 3, 8, width), jnp.float32)
    zero = jnp.zeros((count, width), jnp.float32)

    def modulus(layer, start):
        if layer < 0:
            return received(shared, 0, load_ref[0], start, count)
        return mod_ref[layer, pl.ds(start, count), :]

    def start_block(block, norm):
        start = pl.multiple_of(block * count, count)
        rows = pl.ds(start, count)
        for plane in range(layers):
            total = modulus(plane - 1, start) + modulus(plane, start)
            inverse = inverse_diagonal(free_ref[plane, rows, :], total, edge.at[plane], start, count)
            inv_ref[plane, rows, :] = inverse
            for comp in range(3):
                res = res_ref[comp, plane, rows, :]
                z = inverse * res
                z_ref[plane, comp, rows, :] = z
                norm = norm + res * z
        for comp in range(3):
            under[comp, rows, :] = up_ref[pl.ds(comp * height + start, count), :]
        return norm

    norm = lax.fori_loop(0, height // count, start_block, zero)

    def image_block(block, sums):
        along, across = sums
        start = pl.multiple_of(block * count, count)
        rows = pl.ds(start, count)
        low = plane_modes(under, (), start, count)
        held = None
        for layer in range(layers):
            high = plane_modes(z_ref, (layer,), start, count)
            lower, upper = layer_forces(low, high, modulus(layer - 1, start))
            if layer > 0:
                plane = layer - 1
                lower = {key: lower[key] + held[key] for key in lower}
                for comp in range(3):
                    image = nodal(lower, comp, carry.at[plane], start, count)
                    v = inv_ref[plane, rows, :] * image
                    v_ref[plane, comp, rows, :] = v
                    along = along + image * z_ref[plane, comp, rows, :]
                    across = across + image * v
            held, low = upper, high
        for comp in range(3):
            part_ref[comp, rows, :] = nodal(held, comp, carry.at[layers - 1], start, count)
        return along, across

    along, across = lax.fori_loop(0, height // count, image_block, (zero, zero))
    sums_ref[...] = add_up((norm, along, across))


def above_kernel(
    down_ref, z_ref, low_v_ref, part_ref, inv_ref, mod_ref, low_sums_ref, inv_top_ref, mod_top_ref,
    top_ref, v_ref, sums_ref, over, carry,
):
    layers, height, width = mod_ref.shape
    count = min(ROWS, height)
    carry[:, :, 0:8, :] = jnp.zeros((2, 3, 8, width), jnp.float32)
    over[:, height : height + 8, :] = jnp.zeros((3, 8, width), jnp.float32)
    top_ref[:, height : height + 8, :] = jnp.zeros((3, 8, width), jnp.float32)
    v_ref[:, :, height : height + 8, :] = jnp.zeros((2, 3, 8, width), jnp.float32)
    zero = jnp.zeros((count, width), jnp.float32)

    for comp in range(3):
        top_ref[comp, 0:height, :] = inv_top_ref[...] * down_ref[comp]
        over[comp, 0:height, :] = down_ref[3 + comp]

    def image_block(block, sums):
        along, across = sums
        start = pl.multiple_of(block * count, count)
        rows = pl.ds(start, count)
        low = plane_modes(z_ref, (layers - 1,), start, count)
        high = plane_modes(top_ref, (), start, count)
        lower, held = layer_forces(low, high, mod_ref[layers - 1, rows, :])
        for comp in range(3):
            image = nodal(lower, comp, carry.at[0], start, count) + part_ref[comp, rows, :]
            v = inv_ref[layers - 1, rows, :] * image
            v_ref[0, comp, rows, :] = v
            along = along + image * z_ref[layers - 1, comp, rows, :]
            across = across + image * v
        lower, _ = layer_forces(high, plane_modes(over, (), start, count), mod_top_ref[rows, :])
        lower = {key: lower[key] + held[key] for key in lower}
        for comp in range(3):
            v_ref[1, comp, rows, :] = inv_top_ref[rows, :] * nodal(lower, comp, carry.at[1], start, count)
        return along, across

    along, across = lax.fori_loop(0, height // count, image_block, (zero, zero))

    def energy_block(block, energy):
        start = pl.multiple_of(block * count, count)
        low = None
        for plane in range(layers + 1):
            if plane < layers - 1:
                high = plane_modes(low_v_ref, (plane,), start, count)
            else:
                high = plane_modes(v_ref, (plane - layers + 1,), start, count)
            if plane > 0:
                modes = layer_modes(low, high)
                energy = energy + mod_ref[plane - 1, pl.ds(start, count), :] * paired(modes, stiff(modes))
            low = high
        return energy

    energy = lax.fori_loop(0, height // count, energy_block, zero)
    sums = low_sums_ref[...] + add_up((zero[:8], along, across, energy))
    sums = jnp.sum(sums, axis=1, keepdims=True)
    lane = lax.broadcasted_iota(jnp.int32, (8, width), 1)
    row = lax.broadcasted_iota(jnp.int32, (8, width), 0)
    sums = jnp.sum(jnp.where(lane == row, sums, 0.0), axis=0, keepdims=True)
    sums_ref[...] = jnp.broadcast_to(sums, sums_ref.shape)


def edge_modes(ref, at, block, count, last):
    out = []
    for comp in range(3):
        here = ref[at(comp) + (pl.ds(block * count, count),)]
        if last:
            row = lax.broadcasted_iota(jnp.int32, here.shape, 0)
            below = jnp.where(row == count - 1, 0.0, pltpu.roll(here, count - 1, 0))
        else:
            below = ref[at(comp) + (pl.ds(block * count + 1, count),)]
        level, change = here + below, below - here
        level_next, change_next = next_lane(level), next_lane(change)
        out.append(((level + level_next, change + change_next), (level_next - level, change_next - change)))
    return out


def dot(modes, forces):
    total = None
    for comp in range(3):
        for a in range(2):
            for b in range(2):
                term = modes[comp][a][b] * forces[comp, a, b]
                total = term if total is None else total + term
    return total


def early_kernel(load_ref, z_ref, low_v_ref, disp_ref, scale_ref, mod_ref, *refs):
    early_ref, upper_ref, inv_top_ref, mod_top_ref, edge = refs[-5:]
    shared = refs[:-5]
    layers, height, width = scale_ref.shape
    share = height // len(shared)
    edge[0:8, :] = jnp.zeros((8, width), jnp.float32)
    for start in range(0, height, share):
        rows = slice(start, start + share)
        stiffness = received(shared, 1, load_ref[0], start, share)
        free = received(shared, 2, load_ref[0], start, share)
        mod_top_ref[rows, :] = stiffness
        total = mod_ref[layers - 1, rows, :] + stiffness
        inv_top_ref[rows, :] = inverse_diagonal(free, total, edge, start, share)
    count = min(ROWS, height)
    for block in range(height // count):
        start = block * count
        rows = slice(start, start + count)
        low = None
        for plane in range(layers):
            last = block == height // count - 1
            u = edge_modes(disp_ref, lambda comp: (0, comp, plane), block, count, last)
            z = plane_modes(z_ref, (plane,), start, count)
            v = plane_modes(low_v_ref, (plane,), start, count) if plane < layers - 1 else None
            if plane > 0:
                layer = plane - 1
                lower, upper = layer_forces(low[0], u, scale_ref[layer, rows, :])
                early_ref[0, layer, rows, :] = dot(low[1], lower) + dot(z, upper)
                part = dot(low[2], lower)
                if plane < layers - 1:
                    part = part + dot(v, upper)
                else:
                    for place, key in enumerate(sorted(upper)):
                        upper_ref[place, rows, :] = upper[key]
                early_ref[1, layer, rows, :] = part
            low = (u, z, v)


def term_kernel(
    load_ref, early_ref, upper_ref, z_ref, top_ref, v_ref, disp_ref, above_ref, scale_ref, term_ref
):
    layers, height, width = scale_ref.shape
    loads, share = term_ref.shape[0], term_ref.shape[3]
    keys = [(comp, a, b) for comp in range(3) for a in range(2) for b in range(2)]
    for block in range(loads):
        start = block * share
        rows = slice(start, start + share)
        place = lax.rem(block - load_ref[0] + loads, loads)
        z_low = plane_modes(z_ref, (layers - 1,), start, share)
        v_low = plane_modes(v_ref, (0,), start, share)
        for layer in range(layers - 1):
            term_ref[place, 0, layer] = early_ref[0, layer, rows, :]
            part = early_ref[1, layer, rows, :]
            if layer == layers - 2:
                part = part + dot(v_low, {key: upper_ref[at, rows, :] for at, key in enumerate(keys)})
            term_ref[place, 1, layer] = part
        last = block == loads - 1
        u_low = edge_modes(disp_ref, lambda comp: (0, comp, layers - 1), block, share, last)
        u_high = edge_modes(above_ref, lambda comp: (comp,), block, share, last)
        lower, upper = layer_forces(u_low, u_high, scale_ref[layers - 1, rows, :])
        z_high = plane_modes(top_ref, (), start, share)
        term_ref[place, 0, layers - 1] = dot(z_low, lower) + dot(z_high, upper)
        v_high = plane_modes(v_ref, (1,), start, share)
        term_ref[place, 1, layers - 1] = dot(v_low, lower) + dot(v_high, upper)


def solve_weights(sums_ref, load, loads):
    device = lax.broadcasted_iota(jnp.int32, sums_ref.shape, 0)
    lane = lax.broadcasted_iota(jnp.int32, (1, sums_ref.shape[1]), 1)
    mine = jnp.where(lax.rem(device, loads) == load, sums_ref[...], 0.0)
    mine = jnp.sum(mine, axis=0, keepdims=True)
    norm, along, across, energy = [
        jnp.sum(jnp.where(lane == place, mine, 0.0), axis=1, keepdims=True) for place in range(4)
    ]
    first = norm / along
    later = first * first * across - norm
    second = later / (first * first * (energy - across * across / along))
    return first + second * (first * across / along), second * first


def weight_kernel(loads, load_ref, sums_ref, weight_ref):
    for place in range(loads):
        weights = solve_weights(sums_ref, lax.rem(load_ref[0] - place + loads, loads), loads)
        for which, weight in enumerate(weights):
            weight_ref[2 * place + which] = jnp.broadcast_to(weight, weight_ref.shape[1:])


def finish_kernel(weight_ref, z_ref, low_v_ref, v_ref, *refs):
    term_refs = refs[:-2]
    x_ref, grad_ref = refs[-2:]
    layers, height = x_ref.shape[2], x_ref.shape[3]
    from_z, from_v = weight_ref[0, 0:1, :], weight_ref[1, 0:1, :]
    for comp in range(3):
        for plane in range(layers):
            v = low_v_ref[plane, comp, 0:height] if plane < layers - 1 else v_ref[0, comp, 0:height]
            x_ref[0, comp, plane] = from_z * z_ref[plane, comp, 0:height] - from_v * v
    total = None
    for place, term_ref in enumerate(term_refs):
        part = weight_ref[2 * place, 0:1, :] * term_ref[0] - weight_ref[2 * place + 1, 0:1, :] * term_ref[1]
        total = part if total is None else total + part
    grad_ref[...] = total


def f32(*shape):
    return jax.ShapeDtypeStruct(shape, jnp.float32)


def shards(forward_disp, adjoint_rhs, modulus_factor, zone_base, zone_ids, fixed_mask):
    layers, height, width = modulus_factor.shape
    loads = lax.axis_size("load")
    devices = lax.axis_size("space") * loads
    load = lax.axis_index("load")
    whole = pl.BlockSpec(memory_space=pltpu.VMEM)
    scalar = pl.BlockSpec(memory_space=pltpu.SMEM)
    params = pltpu.CompilerParams(vmem_limit_bytes=12 * 2**20)
    pad = height + 8
    share = height // loads
    position = load.astype(jnp.int32)[None]

    def hbm(*arrays):
        return [pltpu.with_memory_space_constraint(array, pltpu.HBM) for array in arrays]

    far = pl.BlockSpec(memory_space=pltpu.HBM)
    up, part_down, down, lowest, res, modulus, scale, free = pl.pallas_call(
        pack_kernel,
        out_shape=[f32(3 * height + share, width), f32(2 * share, width), f32(6, height, width), f32(3, height, width)]
        + [f32(3, layers, height, width)]
        + [f32(layers, height, width)] * 3,
        in_specs=[scalar] + [far] * 6,
        out_specs=[whole] * 8,
        scratch_shapes=[
            pltpu.SMEM(zone_base.shape, jnp.float32),
            pltpu.VMEM((3, layers, height, width), jnp.float32),
            pltpu.VMEM((layers, height, width), jnp.float32),
            pltpu.VMEM((layers, height, width), jnp.int32),
            pltpu.VMEM((layers, height, width), jnp.int32),
            pltpu.VMEM((2, pad, width), jnp.float32),
            pltpu.SemaphoreType.DMA((6,)),
        ],
        compiler_params=params,
        name="pack",
    )(position, *hbm(zone_base, adjoint_rhs, modulus_factor, zone_ids, fixed_mask, forward_disp))
    from_below = permute(up, "space", 1)
    shared = jnp.concatenate([from_below[3 * height :], permute(part_down, "space", -1)])
    shared = [shared] + [permute(shared, "load", by, wrap=True) for by in range(1, loads)]
    from_above = permute(down, "space", -1)

    z, low_v, part, inverse, low_sums = pl.pallas_call(
        below_kernel,
        out_shape=(
            f32(layers, 3, pad, width),
            f32(layers - 1, 3, pad, width),
            f32(3, height, width),
            f32(layers, height, width),
            f32(8, width),
        ),
        in_specs=[scalar] + [whole] * (4 + loads),
        out_specs=[whole] * 5,
        scratch_shapes=[
            pltpu.VMEM((3, pad, width), jnp.float32),
            pltpu.VMEM((layers, 3, pad, width), jnp.float32),
            pltpu.VMEM((layers, pad, width), jnp.float32),
        ],
        compiler_params=params,
        cost_estimate=pl.CostEstimate(flops=10**9, bytes_accessed=2**10, transcendentals=0),
        name="below",
    )(position, from_below, res, modulus, free, *shared)
    early, upper, inverse_top, modulus_top = pl.pallas_call(
        early_kernel,
        out_shape=(f32(2, layers - 1, height, width), f32(12, height, width), f32(height, width), f32(height, width)),
        in_specs=[scalar] + [whole] * (5 + loads),
        out_specs=[whole] * 4,
        scratch_shapes=[pltpu.VMEM((pad, width), jnp.float32)],
        compiler_params=params,
        name="early",
    )(position, z, low_v, forward_disp, scale, modulus, *shared)
    lowest, early = lax.optimization_barrier((lowest, early))
    above_disp = permute(lowest, "space", -1)

    top, v, sums = pl.pallas_call(
        above_kernel,
        out_shape=(f32(3, pad, width), f32(2, 3, pad, width), f32(devices, 128)),
        in_specs=[whole] * 9,
        out_specs=[whole] * 3,
        scratch_shapes=[
            pltpu.VMEM((3, pad, width), jnp.float32),
            pltpu.VMEM((2, 3, pad, width), jnp.float32),
        ],
        compiler_params=params,
        name="above",
    )(from_above, z, low_v, part, inverse, modulus, low_sums, inverse_top, modulus_top)
    sums = lax.all_to_all(sums, ("space", "load"), 0, 0, tiled=True)

    terms = pl.pallas_call(
        term_kernel,
        out_shape=f32(loads, 2, layers, share, width),
        in_specs=[scalar] + [whole] * 8,
        out_specs=whole,
        compiler_params=params,
        name="term",
    )(position, early, upper, z, top, v, forward_disp, above_disp, scale)
    terms = [terms[0]] + [permute(terms[by], "load", by, wrap=True) for by in range(1, loads)]

    weights = pl.pallas_call(
        functools.partial(weight_kernel, loads),
        out_shape=f32(2 * loads, 8, width),
        in_specs=[scalar, whole],
        out_specs=whole,
        compiler_params=params,
        cost_estimate=pl.CostEstimate(flops=4 * 10**9, bytes_accessed=2**20, transcendentals=0),
        name="weight",
    )(position, sums)
    return pl.pallas_call(
        finish_kernel,
        out_shape=(f32(1, 3, layers, height, width), f32(layers, share, width)),
        in_specs=[whole] * (4 + loads),
        out_specs=[whole] * 2,
        compiler_params=params,
        name="finish",
    )(weights, z, low_v, v, *terms)


def solution(mesh):
    placed = (
        P("load", None, "space", None, None),
        P("load", None, "space", None, None),
        P("space", None, None),
        P(),
        P("space", None, None),
        P("space", None, None),
    )
    return jax.shard_map(
        shards,
        mesh=mesh,
        in_specs=placed,
        out_specs=(P("load", None, "space", None, None), P("space", "load", None)),
        check_vma=False,
    )
```

```python
import functools

import jax
import jax.numpy as jnp
from jax import lax
from jax.experimental import pallas as pl
from jax.experimental.pallas import tpu as pltpu
from jax.sharding import PartitionSpec as P

POISSON = 0.3
SHEAR = 0.5 / (1.0 + POISSON)
RATIO = 2.0 * POISSON / (1.0 - 2.0 * POISSON)
CLASS = [0.0] + [12.0 * SHEAR / 64.0 / 3.0**order for order in (1, 2, 3)]
CORNER = CLASS[1] * (RATIO + 4.0) + CLASS[2] * (2.0 * (RATIO + 3.0) + 2.0) + CLASS[3] * (RATIO + 4.0)
ROWS = 64


def unrolled(low, high, body, carry):
    for step in range(low, high):
        carry = body(step, carry)
    return carry


def permute(shard, axis, by, wrap=False):
    devices = lax.axis_size(axis)
    if wrap:
        pairs = [(i, (i + by) % devices) for i in range(devices)]
    else:
        pairs = [(i, i + by) for i in range(devices) if 0 <= i + by < devices]
    return lax.ppermute(shard, axis, pairs)


def next_lane(value):
    width = value.shape[-1]
    lane = lax.broadcasted_iota(jnp.int32, value.shape, value.ndim - 1)
    return jnp.where(lane == width - 1, 0.0, pltpu.roll(value, width - 1, value.ndim - 1))


def last_lane(value):
    lane = lax.broadcasted_iota(jnp.int32, value.shape, value.ndim - 1)
    return jnp.where(lane == 0, 0.0, pltpu.roll(value, 1, value.ndim - 1))


def plane_modes(ref, at, start, count):
    out = []
    for comp in range(3):
        here = ref[at + (comp, pl.ds(start, count))]
        below = ref[at + (comp, pl.ds(start + 1, count))]
        level, change = here + below, below - here
        level_next, change_next = next_lane(level), next_lane(change)
        out.append(((level + level_next, change + change_next), (level_next - level, change_next - change)))
    return out


def layer_modes(low, high):
    out = []
    for comp in range(3):
        modes = {}
        for a in range(2):
            for b in range(2):
                if a or b:
                    modes[a, b, 0] = low[comp][a][b] + high[comp][a][b]
                modes[a, b, 1] = high[comp][a][b] - low[comp][a][b]
        out.append(modes)
    return out


PAIRS = (((0, (1, 1, 0)), (2, (0, 1, 1))), ((1, (1, 1, 0)), (2, (1, 0, 1))), ((0, (1, 0, 1)), (1, (0, 1, 1))))


def stiff(modes):
    u, v, w = modes
    out = [{}, {}, {}]
    trace = RATIO * (u[1, 0, 0] + v[0, 1, 0] + w[0, 0, 1])
    out[0][1, 0, 0] = trace + 2.0 * u[1, 0, 0]
    out[1][0, 1, 0] = trace + 2.0 * v[0, 1, 0]
    out[2][0, 0, 1] = trace + 2.0 * w[0, 0, 1]
    for (one, at), (two, by) in PAIRS:
        both = RATIO * (modes[one][at] + modes[two][by])
        out[one][at] = both + 3.0 * modes[one][at]
        out[two][by] = both + 3.0 * modes[two][by]
    out[0][0, 1, 0] = out[1][1, 0, 0] = u[0, 1, 0] + v[1, 0, 0]
    out[1][0, 0, 1] = out[2][0, 1, 0] = v[0, 0, 1] + w[0, 1, 0]
    out[2][1, 0, 0] = out[0][0, 0, 1] = w[1, 0, 0] + u[0, 0, 1]
    first = u[0, 1, 1] + v[1, 0, 1]
    second = v[1, 0, 1] + w[1, 1, 0]
    third = w[1, 1, 0] + u[0, 1, 1]
    out[0][0, 1, 1] = first + third
    out[1][1, 0, 1] = first + second
    out[2][1, 1, 0] = second + third
    for comp in range(3):
        out[comp][1, 1, 1] = (RATIO + 4.0) * modes[comp][1, 1, 1]
    return out


def paired(modes, forces):
    total = None
    for order in (1, 2, 3):
        part = None
        for comp in range(3):
            for key, force in forces[comp].items():
                if sum(key) == order:
                    term = modes[comp][key] * force
                    part = term if part is None else part + term
        part = CLASS[order] * part
        total = part if total is None else total + part
    return total


def layer_forces(low, high, stiffness):
    forces = stiff(layer_modes(low, high))
    weight = [None] + [CLASS[order] * stiffness for order in (1, 2, 3)]
    lower, upper = {}, {}
    for comp in range(3):
        for a in range(2):
            for b in range(2):
                change = weight[a + b + 1] * forces[comp][a, b, 1]
                if a or b:
                    level = weight[a + b] * forces[comp][a, b, 0]
                    lower[comp, a, b] = level - change
                    upper[comp, a, b] = level + change
                else:
                    lower[comp, a, b] = -change
                    upper[comp, a, b] = change
    return lower, upper


def nodal(forces, comp, carry, start, count):
    sides = []
    for b in range(2):
        level, change = forces[comp, 0, b], forces[comp, 1, b]
        sides.append(level - change + last_lane(level + change))
    carry[comp, pl.ds(start + 8, count), :] = sides[0] + sides[1]
    return sides[0] - sides[1] + carry[comp, pl.ds(start + 7, count), :]


def add_up(parts):
    row = lax.broadcasted_iota(jnp.int32, (8, parts[0].shape[-1]), 0)
    out = jnp.zeros(row.shape, jnp.float32)
    for place, part in enumerate(parts):
        out = jnp.where(row == place, jnp.sum(part, axis=0, keepdims=True), out)
    return out


def inverse_diagonal(free, total, edge, start, count):
    total = total + last_lane(total)
    edge[pl.ds(start + 8, count), :] = total
    return free / (CORNER * (total + edge[pl.ds(start + 7, count), :]))


def received(shared, item, load, start, count):
    loads, share = len(shared), shared[0].shape[0] // 3
    rows = pl.ds(item * share + start % share, count)
    distance = lax.rem(load - start // share + loads, loads)
    out = shared[0][rows, :]
    for by in range(1, loads):
        out = jnp.where(distance == by, shared[by][rows, :], out)
    return out


def pack_kernel(
    load_ref, base_hbm, rhs_hbm, factor_hbm, ids_hbm, mask_hbm, disp_hbm,
    up_ref, part_ref, down_ref, low_ref, res_ref, mod_ref, scale_ref, free_ref,
    base_ref, rhs_ref, factor_ref, ids_ref, mask_ref, edge, sems,
):
    layers, height, width = factor_ref.shape
    share = part_ref.shape[0] // 2
    mine = pl.ds(pl.multiple_of(load_ref[0] * share, 8), share)
    pairs = (
        (base_hbm, base_ref),
        (ids_hbm, ids_ref),
        (factor_hbm, factor_ref),
        (mask_hbm, mask_ref),
        (rhs_hbm.at[0], rhs_ref),
        (disp_hbm.at[0, :, 0], low_ref),
    )
    copies = [pltpu.make_async_copy(source, target, sems.at[place]) for place, (source, target) in enumerate(pairs)]
    for copy in copies:
        copy.start()
    edge[:, 0:8, :] = jnp.zeros((2, 8, width), jnp.float32)
    for copy in copies[:3]:
        copy.wait()
    scale = jnp.full(ids_ref.shape, base_ref[0])
    for zone in range(1, base_ref.shape[0]):
        scale = jnp.where(ids_ref[...] == zone, base_ref[zone], scale)
    modulus = factor_ref[...] * scale
    scale_ref[...] = scale
    mod_ref[...] = modulus
    copies[3].wait()
    free = 1.0 - mask_ref[...].astype(jnp.float32)
    free_ref[...] = free
    up_ref[3 * height :] = mod_ref[layers - 1, mine, :]
    part_ref[0:share] = mod_ref[0, mine, :]
    part_ref[share:] = free_ref[0, mine, :]
    top = inverse_diagonal(free[layers - 1], modulus[layers - 2] + modulus[layers - 1], edge.at[0], 0, height)
    second = top
    if layers > 2:
        second = inverse_diagonal(free[1], modulus[0] + modulus[1], edge.at[1], 0, height)
    copies[4].wait()
    for comp in range(3):
        res = free * rhs_ref[comp]
        res_ref[comp] = res
        up_ref[comp * height : (comp + 1) * height] = res[layers - 1] * top
        down_ref[comp] = res[0]
        down_ref[3 + comp] = res[1] * second
    copies[5].wait()


def below_kernel(load_ref, up_ref, res_ref, mod_ref, free_ref, *refs):
    z_ref, v_ref, part_ref, inv_ref, sums_ref, under, carry, edge = refs[-8:]
    shared = refs[:-8]
    layers, height, width = mod_ref.shape
    count = min(ROWS, height // len(shared))
    edge[:, 0:8, :] = jnp.zeros((layers, 8, width), jnp.float32)
    carry[:, :, 0:8, :] = jnp.zeros((layers, 3, 8, width), jnp.float32)
    under[:, height : height + 8, :] = jnp.zeros((3, 8, width), jnp.float32)
    z_ref[:, :, height : height + 8, :] = jnp.zeros((layers, 3, 8, width), jnp.float32)
    v_ref[:, :, height : height + 8, :] = jnp.zeros((layers - 1, 3, 8, width), jnp.float32)
    zero = jnp.zeros((count, width), jnp.float32)

    def modulus(layer, start):
        if layer < 0:
            return received(shared, 0, load_ref[0], start, count)
        return mod_ref[layer, pl.ds(start, count), :]

    def start_block(block, norm):
        start = block * count
        rows = pl.ds(start, count)
        for plane in range(layers):
            total = modulus(plane - 1, start) + modulus(plane, start)
            inverse = inverse_diagonal(free_ref[plane, rows, :], total, edge.at[plane], start, count)
            inv_ref[plane, rows, :] = inverse
            for comp in range(3):
                res = res_ref[comp, plane, rows, :]
                z = inverse * res
                z_ref[plane, comp, rows, :] = z
                norm = norm + res * z
        for comp in range(3):
            under[comp, rows, :] = up_ref[pl.ds(comp * height + start, count), :]
        return norm

    norm = unrolled(0, height // count, start_block, zero)

    def image_block(block, sums):
        along, across = sums
        start = block * count
        rows = pl.ds(start, count)
        low = plane_modes(under, (), start, count)
        held = None
        for layer in range(layers):
            high = plane_modes(z_ref, (layer,), start, count)
            lower, upper = layer_forces(low, high, modulus(layer - 1, start))
            if layer > 0:
                plane = layer - 1
                lower = {key: lower[key] + held[key] for key in lower}
                for comp in range(3):
                    image = nodal(lower, comp, carry.at[plane], start, count)
                    v = inv_ref[plane, rows, :] * image
                    v_ref[plane, comp, rows, :] = v
                    along = along + image * z_ref[plane, comp, rows, :]
                    across = across + image * v
            held, low = upper, high
        for comp in range(3):
            part_ref[comp, rows, :] = nodal(held, comp, carry.at[layers - 1], start, count)
        return along, across

    along, across = unrolled(0, height // count, image_block, (zero, zero))
    sums_ref[...] = add_up((norm, along, across))


def above_kernel(
    down_ref, z_ref, low_v_ref, part_ref, inv_ref, mod_ref, low_sums_ref, inv_top_ref, mod_top_ref,
    top_ref, v_ref, sums_ref, over, carry,
):
    layers, height, width = mod_ref.shape
    count = height
    carry[:, :, 0:8, :] = jnp.zeros((2, 3, 8, width), jnp.float32)
    over[:, height : height + 8, :] = jnp.zeros((3, 8, width), jnp.float32)
    top_ref[:, height : height + 8, :] = jnp.zeros((3, 8, width), jnp.float32)
    v_ref[:, :, height : height + 8, :] = jnp.zeros((2, 3, 8, width), jnp.float32)
    zero = jnp.zeros((count, width), jnp.float32)

    for comp in range(3):
        top_ref[comp, 0:height, :] = inv_top_ref[...] * down_ref[comp]
        over[comp, 0:height, :] = down_ref[3 + comp]

    def image_block(block, sums):
        along, across = sums
        start = block * count
        rows = pl.ds(start, count)
        low = plane_modes(z_ref, (layers - 1,), start, count)
        high = plane_modes(top_ref, (), start, count)
        lower, held = layer_forces(low, high, mod_ref[layers - 1, rows, :])
        for comp in range(3):
            image = nodal(lower, comp, carry.at[0], start, count) + part_ref[comp, rows, :]
            v = inv_ref[layers - 1, rows, :] * image
            v_ref[0, comp, rows, :] = v
            along = along + image * z_ref[layers - 1, comp, rows, :]
            across = across + image * v
        lower, _ = layer_forces(high, plane_modes(over, (), start, count), mod_top_ref[rows, :])
        lower = {key: lower[key] + held[key] for key in lower}
        for comp in range(3):
            v_ref[1, comp, rows, :] = inv_top_ref[rows, :] * nodal(lower, comp, carry.at[1], start, count)
        return along, across

    along, across = unrolled(0, height // count, image_block, (zero, zero))

    def energy_block(block, energy):
        start = block * count
        low = None
        for plane in range(layers + 1):
            if plane < layers - 1:
                high = plane_modes(low_v_ref, (plane,), start, count)
            else:
                high = plane_modes(v_ref, (plane - layers + 1,), start, count)
            if plane > 0:
                modes = layer_modes(low, high)
                energy = energy + mod_ref[plane - 1, pl.ds(start, count), :] * paired(modes, stiff(modes))
            low = high
        return energy

    energy = unrolled(0, height // count, energy_block, zero)
    sums = low_sums_ref[...] + add_up((zero[:8], along, across, energy))
    sums = jnp.sum(sums, axis=1, keepdims=True)
    lane = lax.broadcasted_iota(jnp.int32, (8, width), 1)
    row = lax.broadcasted_iota(jnp.int32, (8, width), 0)
    sums = jnp.sum(jnp.where(lane == row, sums, 0.0), axis=0, keepdims=True)
    sums_ref[...] = jnp.broadcast_to(sums, sums_ref.shape)


def edge_modes(ref, at, block, count, last):
    out = []
    for comp in range(3):
        here = ref[at(comp) + (pl.ds(block * count, count),)]
        if last:
            row = lax.broadcasted_iota(jnp.int32, here.shape, 0)
            below = jnp.where(row == count - 1, 0.0, pltpu.roll(here, count - 1, 0))
        else:
            below = ref[at(comp) + (pl.ds(block * count + 1, count),)]
        level, change = here + below, below - here
        level_next, change_next = next_lane(level), next_lane(change)
        out.append(((level + level_next, change + change_next), (level_next - level, change_next - change)))
    return out


def dot(modes, forces):
    total = None
    for comp in range(3):
        for a in range(2):
            for b in range(2):
                term = modes[comp][a][b] * forces[comp, a, b]
                total = term if total is None else total + term
    return total


def early_kernel(load_ref, z_ref, low_v_ref, disp_ref, scale_ref, mod_ref, *refs):
    early_ref, upper_ref, inv_top_ref, mod_top_ref, edge = refs[-5:]
    shared = refs[:-5]
    layers, height, width = scale_ref.shape
    share = height // len(shared)
    edge[0:8, :] = jnp.zeros((8, width), jnp.float32)
    for start in range(0, height, share):
        rows = slice(start, start + share)
        stiffness = received(shared, 1, load_ref[0], start, share)
        free = received(shared, 2, load_ref[0], start, share)
        mod_top_ref[rows, :] = stiffness
        total = mod_ref[layers - 1, rows, :] + stiffness
        inv_top_ref[rows, :] = inverse_diagonal(free, total, edge, start, share)
    count = min(ROWS, height)
    for block in range(height // count):
        start = block * count
        rows = slice(start, start + count)
        low = None
        for plane in range(layers):
            last = block == height // count - 1
            u = edge_modes(disp_ref, lambda comp: (0, comp, plane), block, count, last)
            z = plane_modes(z_ref, (plane,), start, count)
            v = plane_modes(low_v_ref, (plane,), start, count) if plane < layers - 1 else None
            if plane > 0:
                layer = plane - 1
                lower, upper = layer_forces(low[0], u, scale_ref[layer, rows, :])
                early_ref[0, layer, rows, :] = dot(low[1], lower) + dot(z, upper)
                part = dot(low[2], lower)
                if plane < layers - 1:
                    part = part + dot(v, upper)
                else:
                    for place, key in enumerate(sorted(upper)):
                        upper_ref[place, rows, :] = upper[key]
                early_ref[1, layer, rows, :] = part
            low = (u, z, v)


def term_kernel(
    load_ref, early_ref, upper_ref, z_ref, top_ref, v_ref, disp_ref, above_ref, scale_ref, term_ref
):
    layers, height, width = scale_ref.shape
    loads, share = term_ref.shape[0], term_ref.shape[3]
    keys = [(comp, a, b) for comp in range(3) for a in range(2) for b in range(2)]
    for block in range(loads):
        start = block * share
        rows = slice(start, start + share)
        place = lax.rem(block - load_ref[0] + loads, loads)
        z_low = plane_modes(z_ref, (layers - 1,), start, share)
        v_low = plane_modes(v_ref, (0,), start, share)
        for layer in range(layers - 1):
            term_ref[place, 0, layer] = early_ref[0, layer, rows, :]
            part = early_ref[1, layer, rows, :]
            if layer == layers - 2:
                part = part + dot(v_low, {key: upper_ref[at, rows, :] for at, key in enumerate(keys)})
            term_ref[place, 1, layer] = part
        last = block == loads - 1
        u_low = edge_modes(disp_ref, lambda comp: (0, comp, layers - 1), block, share, last)
        u_high = edge_modes(above_ref, lambda comp: (comp,), block, share, last)
        lower, upper = layer_forces(u_low, u_high, scale_ref[layers - 1, rows, :])
        z_high = plane_modes(top_ref, (), start, share)
        term_ref[place, 0, layers - 1] = dot(z_low, lower) + dot(z_high, upper)
        v_high = plane_modes(v_ref, (1,), start, share)
        term_ref[place, 1, layers - 1] = dot(v_low, lower) + dot(v_high, upper)


def solve_weights(sums_ref, load, loads):
    device = lax.broadcasted_iota(jnp.int32, sums_ref.shape, 0)
    lane = lax.broadcasted_iota(jnp.int32, (1, sums_ref.shape[1]), 1)
    mine = jnp.where(lax.rem(device, loads) == load, sums_ref[...], 0.0)
    mine = jnp.sum(mine, axis=0, keepdims=True)
    norm, along, across, energy = [
        jnp.sum(jnp.where(lane == place, mine, 0.0), axis=1, keepdims=True) for place in range(4)
    ]
    first = norm / along
    later = first * first * across - norm
    second = later / (first * first * (energy - across * across / along))
    return first + second * (first * across / along), second * first


def weight_kernel(loads, load_ref, sums_ref, weight_ref):
    for place in range(loads):
        weights = solve_weights(sums_ref, lax.rem(load_ref[0] - place + loads, loads), loads)
        for which, weight in enumerate(weights):
            weight_ref[2 * place + which] = jnp.broadcast_to(weight, weight_ref.shape[1:])


def finish_kernel(weight_ref, z_ref, low_v_ref, v_ref, *refs):
    term_refs = refs[:-2]
    x_ref, grad_ref = refs[-2:]
    layers, height = x_ref.shape[2], x_ref.shape[3]
    from_z, from_v = weight_ref[0, 0:1, :], weight_ref[1, 0:1, :]
    for comp in range(3):
        for plane in range(layers):
            v = low_v_ref[plane, comp, 0:height] if plane < layers - 1 else v_ref[0, comp, 0:height]
            x_ref[0, comp, plane] = from_z * z_ref[plane, comp, 0:height] - from_v * v
    total = None
    for place, term_ref in enumerate(term_refs):
        part = weight_ref[2 * place, 0:1, :] * term_ref[0] - weight_ref[2 * place + 1, 0:1, :] * term_ref[1]
        total = part if total is None else total + part
    grad_ref[...] = total


def f32(*shape):
    return jax.ShapeDtypeStruct(shape, jnp.float32)


def shards(forward_disp, adjoint_rhs, modulus_factor, zone_base, zone_ids, fixed_mask):
    layers, height, width = modulus_factor.shape
    loads = lax.axis_size("load")
    devices = lax.axis_size("space") * loads
    load = lax.axis_index("load")
    whole = pl.BlockSpec(memory_space=pltpu.VMEM)
    scalar = pl.BlockSpec(memory_space=pltpu.SMEM)
    params = pltpu.CompilerParams(vmem_limit_bytes=12 * 2**20)
    pad = height + 8
    share = height // loads
    position = load.astype(jnp.int32)[None]

    def hbm(*arrays):
        return [pltpu.with_memory_space_constraint(array, pltpu.HBM) for array in arrays]

    far = pl.BlockSpec(memory_space=pltpu.HBM)
    up, part_down, down, lowest, res, modulus, scale, free = pl.pallas_call(
        pack_kernel,
        out_shape=[f32(3 * height + share, width), f32(2 * share, width), f32(6, height, width), f32(3, height, width)]
        + [f32(3, layers, height, width)]
        + [f32(layers, height, width)] * 3,
        in_specs=[scalar] + [far] * 6,
        out_specs=[whole] * 8,
        scratch_shapes=[
            pltpu.SMEM(zone_base.shape, jnp.float32),
            pltpu.VMEM((3, layers, height, width), jnp.float32),
            pltpu.VMEM((layers, height, width), jnp.float32),
            pltpu.VMEM((layers, height, width), jnp.int32),
            pltpu.VMEM((layers, height, width), jnp.int32),
            pltpu.VMEM((2, pad, width), jnp.float32),
            pltpu.SemaphoreType.DMA((6,)),
        ],
        compiler_params=params,
        name="pack",
    )(position, *hbm(zone_base, adjoint_rhs, modulus_factor, zone_ids, fixed_mask, forward_disp))
    from_below = permute(up, "space", 1)
    shared = jnp.concatenate([from_below[3 * height :], permute(part_down, "space", -1)])
    shared = [shared] + [permute(shared, "load", by, wrap=True) for by in range(1, loads)]
    from_above = permute(down, "space", -1)

    z, low_v, part, inverse, low_sums = pl.pallas_call(
        below_kernel,
        out_shape=(
            f32(layers, 3, pad, width),
            f32(layers - 1, 3, pad, width),
            f32(3, height, width),
            f32(layers, height, width),
            f32(8, width),
        ),
        in_specs=[scalar] + [whole] * (4 + loads),
        out_specs=[whole] * 5,
        scratch_shapes=[
            pltpu.VMEM((3, pad, width), jnp.float32),
            pltpu.VMEM((layers, 3, pad, width), jnp.float32),
            pltpu.VMEM((layers, pad, width), jnp.float32),
        ],
        compiler_params=params,
        cost_estimate=pl.CostEstimate(flops=10**9, bytes_accessed=2**10, transcendentals=0),
        name="below",
    )(position, from_below, res, modulus, free, *shared)
    early, upper, inverse_top, modulus_top = pl.pallas_call(
        early_kernel,
        out_shape=(f32(2, layers - 1, height, width), f32(12, height, width), f32(height, width), f32(height, width)),
        in_specs=[scalar] + [whole] * (5 + loads),
        out_specs=[whole] * 4,
        scratch_shapes=[pltpu.VMEM((pad, width), jnp.float32)],
        compiler_params=params,
        name="early",
    )(position, z, low_v, forward_disp, scale, modulus, *shared)
    lowest, early = lax.optimization_barrier((lowest, early))
    above_disp = permute(lowest, "space", -1)

    top, v, sums = pl.pallas_call(
        above_kernel,
        out_shape=(f32(3, pad, width), f32(2, 3, pad, width), f32(devices, 128)),
        in_specs=[whole] * 9,
        out_specs=[whole] * 3,
        scratch_shapes=[
            pltpu.VMEM((3, pad, width), jnp.float32),
            pltpu.VMEM((2, 3, pad, width), jnp.float32),
        ],
        compiler_params=params,
        name="above",
    )(from_above, z, low_v, part, inverse, modulus, low_sums, inverse_top, modulus_top)
    sums = lax.all_to_all(sums, ("space", "load"), 0, 0, tiled=True)

    terms = pl.pallas_call(
        term_kernel,
        out_shape=f32(loads, 2, layers, share, width),
        in_specs=[scalar] + [whole] * 8,
        out_specs=whole,
        compiler_params=params,
        name="term",
    )(position, early, upper, z, top, v, forward_disp, above_disp, scale)
    terms = [terms[0]] + [permute(terms[by], "load", by, wrap=True) for by in range(1, loads)]

    weights = pl.pallas_call(
        functools.partial(weight_kernel, loads),
        out_shape=f32(2 * loads, 8, width),
        in_specs=[scalar, whole],
        out_specs=whole,
        compiler_params=params,
        cost_estimate=pl.CostEstimate(flops=4 * 10**9, bytes_accessed=2**20, transcendentals=0),
        name="weight",
    )(position, sums)
    return pl.pallas_call(
        finish_kernel,
        out_shape=(f32(1, 3, layers, height, width), f32(layers, share, width)),
        in_specs=[whole] * (4 + loads),
        out_specs=[whole] * 2,
        compiler_params=params,
        name="finish",
    )(weights, z, low_v, v, *terms)


def solution(mesh):
    placed = (
        P("load", None, "space", None, None),
        P("load", None, "space", None, None),
        P("space", None, None),
        P(),
        P("space", None, None),
        P("space", None, None),
    )
    return jax.shard_map(
        shards,
        mesh=mesh,
        in_specs=placed,
        out_specs=(P("load", None, "space", None, None), P("space", "load", None)),
        check_vma=False,
    )
```
